512 devices in a mesh: dp: 16 (over x, y_hi), ep: 32 (over y_lo, z, core).
Axes of the slice: x: 4, y: 8 (y_hi: 4, y_lo: 2; y = y_hi * 2 + y_lo), z: 8, core: 2. Of those that a mesh axis runs over, the one named last changes fastest.
Arguments:
- expert_inputs: bfloat16 [163840, 3584], P(('dp', 'ep')), may hold values from -6 to 6
- hidden_grads: bfloat16 [163840, 256], P(('dp', 'ep')), may hold values from -3 to 3
- row_counts: int32 [16384], P(('dp', 'ep')), may hold values from 0 to 10, as said below
- top_ids: int32 [65536, 8], P(('dp', 'ep')), may hold values from 0 to 383, as said below
- route_slots: int32 [65536, 8], P(('dp', 'ep')), may hold values from -1 to 9, as said below
- master_weights: float32 [32, 3584, 256], P('ep', 'dp'), may hold values from -0.125 to 0.125
- first_moment: float32 [32, 3584, 256], P('ep', 'dp'), may hold values from -6 to 6
- second_moment: float32 [32, 3584, 256], P('ep', 'dp'), may hold values from 0.05 to 2
Outputs:
- input_grads: bfloat16 [65536, 3584], P(('dp', 'ep'))
- new_master: float32 [32, 3584, 256], P('ep', 'dp')
- new_first: float32 [32, 3584, 256], P('ep', 'dp')
- new_second: float32 [32, 3584, 256], P('ep', 'dp')
The draws below stay inside these ranges and needn't reach their ends.
Inputs may be any that keep to these rules, and one draw needn't show every extreme that they name: `row_counts`: row counts of each (replica, expert, source device) block; equal on the 8 devices of one expert, equal to the number of that source's routes to that expert with route_slots >= 0, and 10 is reached in every draw. `top_ids`: each token names 8 different experts; only ids below 4 lie in the window. `route_slots`: -1 for routes outside the window or over capacity; a source device's kept routes to one expert take rows 0 to count - 1 in token order.
All inputs are finite; a program needn't handle non-finite values.
Results may differ from the reference program's by a relative error of at most 0.02.
Values may be sent and summed in bfloat16 or wider, within the bound.
A program may use at most 64 MiB of HBM per device.

```python
import math
import jax
import jax.numpy as jnp
from jax import lax

D = 3584
HIDDEN_SIZE = 2048
HID_DEV = 256
ROUTED = 384
TOP = 8
TOK_DEV = 128
CAP = 10
SLICES = 8
EXPERTS = 4
TOKENS = 65536
N_DP = 16
N_EP = 32


def routing(key):
    groups = EXPERTS * SLICES
    blocks = TOKENS // TOK_DEV
    replicas = blocks // groups
    scores = jax.random.randint(key, (TOKENS, ROUTED), 0, 2 ** 20, dtype=jnp.int32) * 512
    column = lax.broadcasted_iota(jnp.int32, (TOKENS, ROUTED), 1)
    scores = scores + column
    token_index = jnp.arange(TOKENS, dtype=jnp.int32)
    local_index = token_index % TOK_DEV
    source = token_index // TOK_DEV % groups
    plant = (local_index < CAP)[:, None] & (column == (source % EXPERTS)[:, None])
    scores = scores + jnp.where(plant, 2 ** 30, 0).astype(jnp.int32)
    top_scores, chosen = lax.top_k(scores, TOP)
    chosen = chosen.astype(jnp.int32)
    hits = jnp.any(chosen[:, :, None] == jnp.arange(EXPERTS, dtype=jnp.int32)[None, None, :], axis=1).astype(jnp.int32)
    hits = hits.reshape(blocks, TOK_DEV, EXPERTS)
    position = jnp.cumsum(hits, axis=1) - hits
    totals = jnp.minimum(jnp.sum(hits, axis=1), CAP)
    position = position.reshape(TOKENS, EXPERTS)
    inside = chosen < EXPERTS
    safe_ids = jnp.where(inside, chosen, 0)
    picked = jnp.take_along_axis(position, safe_ids, axis=1)
    slot_ids = jnp.where(inside & (picked < CAP), picked, -1).astype(jnp.int32)
    per_source = totals.reshape(replicas, groups, EXPERTS)
    per_slice = jnp.repeat(per_source, SLICES, axis=2)
    counts = jnp.transpose(per_slice, (0, 2, 1)).reshape(replicas * groups * groups).astype(jnp.int32)
    return (chosen, slot_ids, counts)


def draw_row_counts(key, part):
    chosen, slot_ids, counts = routing(key)
    return counts


def draw_top_ids(key, part):
    chosen, slot_ids, counts = routing(key)
    return chosen


def draw_route_slots(key, part):
    chosen, slot_ids, counts = routing(key)
    return slot_ids


def shard_levels(rng, extent, split, low, largest):
    gain = 1.0
    for axis_at, blocks in split:
        steps = jax.random.uniform(jax.random.fold_in(jax.random.fold_in(rng, 6), axis_at), (blocks,), jnp.float32, low / len(split), largest / len(split))
        gain = gain * jnp.repeat(jnp.exp(steps), extent[axis_at] // blocks).reshape((-1,) + (1,) * (len(extent) - 1 - axis_at))
    return gain


def scatter_about(own_key, extent, deviation, bound, cuts=(), held_as=jnp.bfloat16):
    level = shard_levels(own_key, extent, cuts, -0.22, 0.18) if cuts else 1.0
    entries = jax.random.normal(own_key, extent, jnp.float32) * deviation * level
    return jnp.minimum(jnp.maximum(entries, -bound), bound).astype(held_as)


def setup_inputs(seed: int = 0) -> dict:
    arg_keys = jax.random.split(jax.random.key(seed), 9)
    return {
        "expert_inputs": scatter_about(arg_keys[0], (N_DP * N_EP * N_EP * CAP, D), 1.0, 6.0, ((0, 512),)),
        "hidden_grads": scatter_about(arg_keys[1], (N_DP * N_EP * N_EP * CAP, HID_DEV), 0.5, 3.0, ((0, 512),)),
        "row_counts": draw_row_counts(jax.random.fold_in(arg_keys[8], 71), 0),
        "top_ids": draw_top_ids(jax.random.fold_in(arg_keys[8], 71), 0),
        "route_slots": draw_route_slots(jax.random.fold_in(arg_keys[8], 71), 0),
        "master_weights": scatter_about(arg_keys[5], (N_EP, D, HID_DEV), HIDDEN_SIZE ** -0.5, 0.125, ((0, 32), (1, 16)), jnp.float32),
        "first_moment": scatter_about(arg_keys[6], (N_EP, D, HID_DEV), 1.0, 6.0, ((0, 32), (1, 16)), jnp.float32),
        "second_moment": jnp.clip(jnp.exp(math.log(2.0) - 3.6888794 * jax.random.uniform(arg_keys[7], (N_EP, D, HID_DEV), jnp.float32) ** shard_levels(arg_keys[7], (N_EP, D, HID_DEV), ((0, 32), (1, 16)), -0.2, 0.2)), 0.05, 2.0),
    }


beta_one = 0.9
beta_two = 0.999
learn_rate = 0.001
adam_epsilon = 1e-08
weight_decay = 0.1
step_count = 100

def reference(expert_inputs, hidden_grads, row_counts, top_ids, route_slots, master_weights, first_moment, second_moment):
    groups = N_EP
    replicas = N_DP
    capacity = CAP
    current_bf = master_weights.astype(jnp.bfloat16)
    inputs_all = expert_inputs.reshape(replicas, groups, groups * capacity, D)
    grads_all = hidden_grads.reshape(replicas, groups, groups * capacity, HID_DEV)
    live_rows = jnp.arange(capacity, dtype=jnp.int32)[None, None, None, :] < row_counts.reshape(replicas, groups, groups)[:, :, :, None]
    live_rows = live_rows.reshape(replicas, groups, groups * capacity, 1)
    masked_grads = jnp.where(live_rows, grads_all, jnp.zeros_like(grads_all))

    def weight_grad(index):
        rows_in = inputs_all[:, index].reshape(replicas * groups * capacity, D)
        rows_grad = masked_grads[:, index].reshape(replicas * groups * capacity, HID_DEV)
        return lax.dot_general(rows_in, rows_grad, (((0,), (0,)), ((), ())), preferred_element_type=jnp.float32)
    weight_grads = lax.map(weight_grad, jnp.arange(groups, dtype=jnp.int32))
    new_first = beta_one * first_moment + (1.0 - beta_one) * weight_grads
    new_second = beta_two * second_moment + (1.0 - beta_two) * weight_grads * weight_grads
    first_hat = new_first / (1.0 - beta_one ** step_count)
    second_hat = new_second / (1.0 - beta_two ** step_count)
    new_master = master_weights - learn_rate * (first_hat / (jnp.sqrt(second_hat) + adam_epsilon) + weight_decay * master_weights)
    ids_all = top_ids.reshape(replicas, groups * TOK_DEV, TOP)
    slots_all = route_slots.reshape(replicas, groups * TOK_DEV, TOP)
    owner = jnp.arange(groups * TOK_DEV, dtype=jnp.int32) // TOK_DEV

    def replica_grads(operands):
        grads_rep, ids_rep, slots_rep = operands

        def slice_part(index):
            return jnp.dot(grads_rep[index], current_bf[index].T, preferred_element_type=jnp.float32).astype(jnp.bfloat16)
        parts = lax.map(slice_part, jnp.arange(groups, dtype=jnp.int32))
        summed = lax.optimization_barrier(jnp.sum(parts.astype(jnp.float32).reshape(EXPERTS, SLICES, groups * capacity, D), axis=1))
        flat_rows = summed.reshape(EXPERTS * groups * capacity, D)
        total = jnp.zeros((groups * TOK_DEV, D), jnp.float32)
        for route in range(TOP):
            expert_id = ids_rep[:, route]
            slot_id = slots_rep[:, route]
            in_use = slot_id >= 0
            row_index = jnp.where(in_use, (expert_id * groups + owner) * capacity + slot_id, 0).astype(jnp.int32)
            picked = jnp.take(flat_rows, row_index, axis=0)
            total = total + jnp.where(in_use[:, None], picked, jnp.zeros_like(picked))
        return total.astype(jnp.bfloat16)
    input_grads = lax.map(replica_grads, (grads_all, ids_all, slots_all)).reshape(TOKENS, D)
    return (input_grads, new_master, new_first, new_second)
```

```python
import jax
import jax.numpy as jnp
from jax import lax
from jax.experimental import pallas as pl
from jax.experimental.pallas import tpu as pltpu
from jax.sharding import PartitionSpec as P

MESH = pl.DeviceIdType.MESH
F32 = jnp.float32
BF16 = jnp.bfloat16
I32 = jnp.int32

beta_one = 0.9
beta_two = 0.999
learn_rate = 0.001
adam_epsilon = 1e-08
weight_decay = 0.1
step_count = 100

D = 3584
H = 256
SH = 224
CH = 896
CAP = 10
ROWS = 320
BL = 48
N_SEM = 64


def kernel(
    x_ref, hg_ref, cnt_ref, ids_ref, slots_ref, mw_ref, m1_ref, m2_ref,
    out_ref, nw_ref, n1_ref, n2_ref,
    wown, wbuf, hgp, res, rcv1, rcv2, outg, fin,
    sopp, sside, rx1, rx2, ysopp, ysside, ry1, ry2, gown,
    ssem, rsem,
):
    dp = lax.axis_index("dp")
    ep = lax.axis_index("ep")
    x, y = dp // 4, dp % 4
    yl, z, c = ep // 16, (ep // 2) % 8, ep % 2
    odd = z % 2
    sgn = 2 * odd - 1
    sib = 1 - c
    xs = ((x + 1) % 4, (x + 3) % 4)
    ys = ((y + 1) % 4, (y + 3) % 4)
    x2, y2 = (x + 2) % 4, (y + 2) % 4

    def dev(xx=None, yy=None, ll=None, zz=None, cc=None):
        xx = x if xx is None else xx
        yy = y if yy is None else yy
        ll = yl if ll is None else ll
        zz = z if zz is None else zz
        cc = c if cc is None else cc
        return {"dp": xx * 4 + yy, "ep": ll * 16 + zz * 2 + cc}

    place = {}
    used = [0]

    def sem(name, many=1):
        if name not in place:
            place[name] = used[0]
            used[0] += many
        return place[name]

    def copy(src, dst, at, to, landing=None):
        return pltpu.make_async_remote_copy(
            src_ref=src, dst_ref=dst, send_sem=ssem.at[at], recv_sem=rsem.at[at if landing is None else landing],
            device_id=to, device_id_type=MESH,
        )

    def arrived(dst, at):
        copy(dst, dst, at, dev(cc=sib)).wait_recv()

    def sent(src, at):
        copy(src, src, at, dev(cc=sib)).wait_send()

    def send(src, dst, at, to, landing=None):
        copy(src, dst, at, to, landing).start()

    barrier = pltpu.get_barrier_semaphore()
    near = [dev(cc=sib), dev(xx=xs[0]), dev(xx=xs[1])]
    near += [dev(yy=yy, cc=cc) for yy in ys for cc in (c, sib)]
    near += [dev(zz=(z + t) % 8) for t in (1, 2, 3, 5, 6, 7)]
    near += [dev(ll=1 - yl), dev(ll=1 - yl, cc=sib)]
    for to in near:
        pl.semaphore_signal(barrier, inc=1, device_id=to, device_id_type=MESH)

    wown[...] = mw_ref[...].astype(BF16)
    own_core = x % 2
    is_a = c == own_core
    not_a = c != own_core
    slot_x, slot_o = x // 2, x2 // 2
    slot_s = (xs[0] // 2, xs[1] // 2)

    @pl.when(is_a)
    def _():
        wbuf[slot_x, y, c] = wown[...]

    row = lax.broadcasted_iota(I32, (ROWS, 32), 0)
    blk = lax.broadcasted_iota(I32, (ROWS, 32), 1)
    within = row - CAP * blk
    alive = (within >= 0) & (within < jnp.minimum(cnt_ref[...], CAP))
    alive = jnp.sum(jnp.where(alive, 1.0, 0.0), axis=1, keepdims=True) > 0.5
    masked = jnp.where(alive, hg_ref[...].astype(F32), 0.0).astype(BF16)

    b3 = lax.broadcasted_iota(I32, (8, BL, 1), 0)
    w3 = lax.broadcasted_iota(I32, (8, BL, 1), 1)
    l3 = jnp.where(w3 >= 20, 1, 0)
    u3 = w3 - 20 * l3
    c3 = jnp.where(u3 >= 10, 1, 0)
    p3 = u3 - 10 * c3
    z3 = (jnp.where(b3 < 4, z + sgn * b3, z - sgn * (b3 - 3)) + 16) & 7
    source = jnp.where(w3 < 40, (l3 * 16 + z3 * 2 + c3) * CAP + p3, -1).reshape(8 * BL, 1)
    perm = jnp.where(lax.broadcasted_iota(I32, (8 * BL, ROWS), 1) == source, 1.0, 0.0).astype(BF16)
    hgp[c] = jnp.dot(perm, hg_ref[...], preferred_element_type=F32).astype(BF16)

    def dw_chunk(at):
        cols = pl.ds(pl.multiple_of(at * CH, 128), CH)
        return lax.dot_general(x_ref[:, cols], masked, (((0,), (0,)), ((), ())), preferred_element_type=F32)

    pl.semaphore_wait(barrier, len(near))

    s_wy = [sem("wy_up", 2), sem("wy_down", 2)]
    s_wsib = sem("wsib")
    for k in (0, 1):
        send(wown, wbuf.at[slot_x, y, c], s_wy[k] + c, dev(yy=ys[k], cc=own_core))

    @pl.when(not_a)
    def _():
        send(wown, wbuf.at[slot_x, y, c], s_wsib, dev(cc=sib))

    s_hg = sem("hg")
    send(hgp.at[c], hgp.at[c], s_hg, dev(cc=sib))

    s_rx1 = [sem("rx1_right"), sem("rx1_left")]
    sopp[...] = dw_chunk(x2).astype(BF16).reshape(2, CH // 2, H)
    for k in (0, 1):
        send(sopp.at[k], rx1.at[k], s_rx1[k], dev(xx=xs[k]))
    for k in (0, 1):
        sside[k] = dw_chunk(xs[k]).astype(BF16).reshape(2, CH // 2, H)
    gown[...] = dw_chunk(x).reshape(4, SH, H)

    s_wyf = [sem("wyf_up"), sem("wyf_down")]
    s_wx = [sem("wx_right", 4), sem("wx_left", 4)]
    s_wxf = sem("wxf", 4)
    half = SH // 2
    order = (0, 3, 1, 2)
    forward = (0, 0, 1, 1)

    def yat(d):
        return (y + d) % 4

    def spread(d):
        for k in (0, 1):
            block = wbuf.at[slot_x, yat(d)]
            send(block, block, s_wx[k] + d, dev(xx=xs[k]))

    @pl.when(is_a)
    def _():
        arrived(wbuf.at[slot_x, y, sib], s_wsib)
        spread(0)
        for k, d in ((0, 3), (1, 1)):
            for s in (0, 1):
                arrived(wbuf.at[slot_x, yat(d), s], s_wy[k] + s)
            part = wbuf.at[slot_x, yat(d), :, pl.ds(k * half, half)]
            send(part, part, s_wyf[k], dev(yy=ys[k]))
            spread(d)
        for k in (0, 1):
            arrived(wbuf.at[slot_x, y2, :, pl.ds(k * half, half)], s_wyf[k])
        spread(2)

    @pl.when(not_a)
    def _():
        for d in order:
            for k in (0, 1):
                block = wbuf.at[slot_s[1 - k], yat(d)]
                arrived(block, s_wx[k] + d)
                if forward[d] == k:
                    send(block, block, s_wxf + d, dev(xx=xs[k]))

    first = jnp.where(is_a, slot_x, slot_s[1])
    chunk = (2 * first + c, 2 * (1 - first) + c)
    slot = (first, 1 - first)
    arrived(hgp.at[sib], s_hg)

    s_r1 = sem("rows1", 2)
    s_r2 = sem("rows2", 8)
    s_fin = sem("fin", 8)

    def rows_one(i):
        total = jnp.zeros((8 * BL, CH), F32)
        for s in (0, 1):
            total += lax.dot_general(
                hgp[s], wbuf[slot[i], :, s].reshape(CH, H), (((1,), (1,)), ((), ())), preferred_element_type=F32
            )
        res[i] = total.astype(BF16).reshape(8, BL, CH)
        send(res.at[i, pl.ds(4, 4)], rcv1.at[i], s_r1 + i, dev(zz=(z - sgn + 8) % 8))

    def rows_two(i):
        arrived(rcv1.at[i], s_r1 + i)
        for t in (3, 2, 1, 0):
            both = (res[i, t].astype(F32) + rcv1[i, t].astype(F32)).astype(BF16)
            if t == 0:
                rcv2[i, 0] = both
            else:
                res[i, t] = both
                send(res.at[i, t], rcv2.at[i, t], s_r2 + 4 * i + t, dev(zz=(z + sgn * t + 8) % 8))

    rr = lax.broadcasted_iota(I32, (128, 4 * BL), 0)
    col = lax.broadcasted_iota(I32, (1, 4 * BL), 1)
    tt = jnp.zeros_like(col)
    for t in (1, 2, 3):
        tt = tt + jnp.where(col >= t * BL, 1, 0)
    ww = col - BL * tt
    gg = jnp.zeros_like(col)
    for g in (1, 2, 3):
        gg = gg + jnp.where(ww >= g * CAP, 1, 0)
    expert = jnp.zeros_like(col)
    for t in range(4):
        step = -sgn * t if t % 2 == 0 else sgn * t
        expert = jnp.where(tt == t, ((z + step + 8) % 8) // 4, expert)
    target = jnp.where(ww < 40, gg * 32 + expert * CAP + ww - CAP * gg, -1)
    sorting = jnp.where(rr == target, 1.0, 0.0).astype(BF16)
    owners = ((1 - yl, c), (1 - yl, sib), (yl, sib))

    def rows_three(i):
        for t in (1, 2, 3):
            arrived(rcv2.at[i, t], s_r2 + 4 * i + t)
        rows = jnp.dot(sorting, rcv2[i].reshape(4 * BL, CH), preferred_element_type=F32)
        outg[i] = rows.astype(BF16).reshape(4, 32, CH)
        for k, (ll, cc) in enumerate(owners):
            send(outg.at[i, ll * 2 + cc], fin.at[chunk[i], yl], s_fin + 3 * i + k, dev(ll=ll, cc=cc),
                 s_fin + 2 * chunk[i] + yl)
        fin[chunk[i], yl] = outg[i, yl * 2 + c]

    s_rx2 = [sem("rx2_right"), sem("rx2_left")]
    s_ry1 = [sem("ry1_up"), sem("ry1_down")]
    s_ry2 = [sem("ry2_up"), sem("ry2_down")]

    def grads_two():
        for k in (0, 1):
            arrived(rx1.at[k], s_rx1[k])
            sside[k, k] = (sside[k, k].astype(F32) + rx1[k].astype(F32)).astype(BF16)
            send(sside.at[k], rx2.at[k], s_rx2[k], dev(xx=xs[k]))

    def grads_three():
        for k in (0, 1):
            arrived(rx2.at[k], s_rx2[k])

        def over_x(at):
            rows = gown[at]
            for k in (0, 1):
                rows = rows + rx2[k, at // 2, pl.ds(pl.multiple_of((at % 2) * SH, 16), SH)].astype(F32)
            return rows

        ysopp[...] = over_x(y2).astype(BF16).reshape(2, SH // 2, H)
        for k in (0, 1):
            send(ysopp.at[k], ry1.at[k], s_ry1[k], dev(yy=ys[k]))
        for k in (0, 1):
            ysside[k] = over_x(ys[k]).astype(BF16).reshape(2, SH // 2, H)
        gown[y] = over_x(y)

    def grads_four():
        for k in (0, 1):
            arrived(ry1.at[k], s_ry1[k])
            ysside[k, k] = (ysside[k, k].astype(F32) + ry1[k].astype(F32)).astype(BF16)
            send(ysside.at[k], ry2.at[k], s_ry2[k], dev(yy=ys[k]))

    def adam():
        for k in (0, 1):
            arrived(ry2.at[k], s_ry2[k])
        grads = gown[y] + ry2[0].reshape(SH, H).astype(F32) + ry2[1].reshape(SH, H).astype(F32)
        master = mw_ref[...]
        new_first = beta_one * m1_ref[...] + (1.0 - beta_one) * grads
        new_second = beta_two * m2_ref[...] + (1.0 - beta_two) * grads * grads
        first_hat = new_first / (1.0 - beta_one**step_count)
        second_hat = new_second / (1.0 - beta_two**step_count)
        nw_ref[...] = master - learn_rate * (
            first_hat / (jnp.sqrt(second_hat) + adam_epsilon) + weight_decay * master
        )
        n1_ref[...] = new_first
        n2_ref[...] = new_second

    rows_one(0)
    grads_two()
    rows_two(0)

    @pl.when(is_a)
    def _():
        for d in order:
            arrived(wbuf.at[slot_o, yat(d)], s_wxf + d)

    rows_one(1)
    grads_three()
    rows_three(0)
    rows_two(1)
    grads_four()
    rows_three(1)
    adam()

    wanted = lax.broadcasted_iota(I32, (64, 128), 0)
    table = jnp.zeros((64, 128), F32)
    for r in range(ids_ref.shape[0]):
        expert_id = ids_ref[pl.ds(r, 1), :]
        slot_id = slots_ref[pl.ds(r, 1), :]
        lower = jnp.where(expert_id >= 2, 1, 0)
        code = lower * 32 + (expert_id - 2 * lower) * CAP + slot_id
        code = jnp.where((slot_id >= 0) & (expert_id < 4), code, -1)
        table = table + jnp.where(wanted == code, 1.0, 0.0)
    table = table.astype(BF16)

    for at in range(4):
        arrived(fin.at[at, 1 - yl], s_fin + 2 * at + 1 - yl)

        @pl.when(c != at % 2)
        def _():
            arrived(fin.at[at, yl], s_fin + 2 * at + yl)

        out_ref[:, pl.ds(at * CH, CH)] = lax.dot_general(
            table, fin[at].reshape(64, CH), (((0,), (0,)), ((), ())), preferred_element_type=F32
        ).astype(BF16)

    for k in (0, 1):
        sent(wown, s_wy[k] + c)
        sent(sopp.at[k], s_rx1[k])
        sent(sside.at[k], s_rx2[k])
        sent(ysopp.at[k], s_ry1[k])
        sent(ysside.at[k], s_ry2[k])
        sent(res.at[k, pl.ds(4, 4)], s_r1 + k)
        for t in (1, 2, 3):
            sent(res.at[k, t], s_r2 + 4 * k + t)
            sent(outg.at[k, t], s_fin + 3 * k + t - 1)
    sent(hgp.at[c], s_hg)

    @pl.when(is_a)
    def _():
        for k, d in ((0, 3), (1, 1)):
            sent(wbuf.at[slot_x, yat(d), :, pl.ds(k * half, half)], s_wyf[k])
        for d in order:
            for k in (0, 1):
                sent(wbuf.at[slot_x, yat(d)], s_wx[k] + d)

    @pl.when(not_a)
    def _():
        sent(wown, s_wsib)
        for d in order:
            sent(wbuf.at[slot_s[1 - forward[d]], yat(d)], s_wxf + d)


def body(expert_inputs, hidden_grads, row_counts, top_ids, route_slots, master, first, second):
    vmem = pl.BlockSpec(memory_space=pltpu.VMEM)
    shard = jax.ShapeDtypeStruct((SH, H), F32)
    out, new_master, new_first, new_second = pl.pallas_call(
        kernel,
        out_shape=(jax.ShapeDtypeStruct((128, D), BF16), shard, shard, shard),
        in_specs=[vmem] * 8,
        out_specs=(vmem,) * 4,
        scratch_shapes=[
            pltpu.VMEM((SH, H), BF16),
            pltpu.VMEM((2, 4, 2, SH, H), BF16),
            pltpu.VMEM((2, 8 * BL, H), BF16),
            pltpu.VMEM((2, 8, BL, CH), BF16),
            pltpu.VMEM((2, 4, BL, CH), BF16),
            pltpu.VMEM((2, 4, BL, CH), BF16),
            pltpu.VMEM((2, 4, 32, CH), BF16),
            pltpu.VMEM((4, 2, 32, CH), BF16),
            pltpu.VMEM((2, CH // 2, H), BF16),
            pltpu.VMEM((2, 2, CH // 2, H), BF16),
            pltpu.VMEM((2, CH // 2, H), BF16),
            pltpu.VMEM((2, 2, CH // 2, H), BF16),
            pltpu.VMEM((2, SH // 2, H), BF16),
            pltpu.VMEM((2, 2, SH // 2, H), BF16),
            pltpu.VMEM((2, SH // 2, H), BF16),
            pltpu.VMEM((2, 2, SH // 2, H), BF16),
            pltpu.VMEM((4, SH, H), F32),
            pltpu.SemaphoreType.DMA((N_SEM,)),
            pltpu.SemaphoreType.DMA((N_SEM,)),
        ],
        compiler_params=pltpu.CompilerParams(
            collective_id=0, has_side_effects=True, vmem_limit_bytes=48 * 2**20
        ),
    )(
        expert_inputs, hidden_grads, row_counts.reshape(1, 32), top_ids.T, route_slots.T,
        master[0], first[0], second[0],
    )
    return out, new_master[None], new_first[None], new_second[None]


def solution(mesh):
    rows = P(("dp", "ep"), None)
    weights = P("ep", "dp", None)
    return jax.shard_map(
        body,
        mesh=mesh,
        in_specs=(rows, rows, P(("dp", "ep")), rows, rows, weights, weights, weights),
        out_specs=(rows, weights, weights, weights),
        check_vma=False,
    )
```

```python
import jax
import jax.numpy as jnp
from jax import lax
from jax.experimental import pallas as pl
from jax.experimental.pallas import tpu as pltpu
from jax.sharding import PartitionSpec as P

MESH = pl.DeviceIdType.MESH
F32 = jnp.float32
BF16 = jnp.bfloat16
I32 = jnp.int32

beta_one = 0.9
beta_two = 0.999
learn_rate = 0.001
adam_epsilon = 1e-08
weight_decay = 0.1
step_count = 100

D = 3584
H = 256
SH = 224
CH = 896
CAP = 10
ROWS = 320
BL = 80
N_SEM = 128
UNITS = (((0, 0, 224), (1, 0, 208), (3, 0, 208)), ((1, 208, 16), (3, 208, 16), (2, 0, 224)))
WIDTHS = tuple(sum(n for _, _, n in unit) for unit in UNITS)
PLACES = (0, WIDTHS[0])


def kernel(
    x_hbm, hg_hbm, cnt_hbm, ids_hbm, slots_hbm, mw_hbm, m1_hbm, m2_hbm,
    out_ref, nw_ref, n1_ref, n2_ref,
    x_ref, hg_ref, cnt_ref, ids_ref, slots_ref, mw_ref, m1_ref, m2_ref,
    wown, wbuf, hgall, hgp, place, sopp, sside, rx1, rx2, ysopp, ysside, ry1, ry2, gown,
    ssem, rsem, lsem, *by_unit,
):
    n_units = len(UNITS)
    res, rcv1, rcv2, outg, fin = (by_unit[n_units * n : n_units * (n + 1)] for n in range(5))

    dp = lax.axis_index("dp")
    ep = lax.axis_index("ep")
    x, y = dp // 4, dp % 4
    yl, z, c = ep // 16, (ep // 2) % 8, ep % 2
    odd = z % 2
    sgn = 2 * odd - 1
    sib = 1 - c
    xs = ((x + 1) % 4, (x + 3) % 4)
    ys = ((y + 1) % 4, (y + 3) % 4)
    x2, y2 = (x + 2) % 4, (y + 2) % 4
    xp = x + 1 - 2 * (x % 2)
    xw = 3 - x

    def dev(xx=None, yy=None, ll=None, zz=None, cc=None):
        xx = x if xx is None else xx
        yy = y if yy is None else yy
        ll = yl if ll is None else ll
        zz = z if zz is None else zz
        cc = c if cc is None else cc
        return {"dp": xx * 4 + yy, "ep": ll * 16 + zz * 2 + cc}

    spots = {}
    used = [0]

    def sem(name, many=1):
        if name not in spots:
            spots[name] = used[0]
            used[0] += many
        return spots[name]

    def copy(src, dst, at, to, landing=None):
        return pltpu.make_async_remote_copy(
            src_ref=src, dst_ref=dst, send_sem=ssem.at[at], recv_sem=rsem.at[at if landing is None else landing],
            device_id=to, device_id_type=MESH,
        )

    def arrived(dst, at):
        copy(dst, dst, at, dev(cc=sib)).wait_recv()

    def sent(src, at):
        copy(src, src, at, dev(cc=sib)).wait_send()

    def send(src, dst, at, to, landing=None):
        copy(src, dst, at, to, landing).start()

    barrier = pltpu.get_barrier_semaphore()
    near = [dev(cc=sib), dev(xx=xs[0]), dev(xx=xs[1])]
    near += [dev(yy=yy, cc=cc) for yy in ys for cc in (c, sib)]
    near += [dev(zz=(z + t) % 8) for t in (1, 2, 3, 5, 6, 7)]
    near += [dev(xx=xp, cc=sib), dev(xx=xw, cc=sib)]
    near += [dev(xx=xx, ll=1 - yl, cc=cc) for xx in (x, xp) for cc in (c, sib)]
    for to in near:
        pl.semaphore_signal(barrier, inc=1, device_id=to, device_id_type=MESH)

    loads = {}
    pairs = (
        ("mw", mw_hbm, mw_ref), ("hg", hg_hbm, hg_ref), ("cnt", cnt_hbm, cnt_ref), ("x", x_hbm, x_ref),
        ("ids", ids_hbm, ids_ref), ("slots", slots_hbm, slots_ref), ("m1", m1_hbm, m1_ref), ("m2", m2_hbm, m2_ref),
    )
    for n, (name, there, here) in enumerate(pairs):
        loads[name] = pltpu.make_async_copy(there, here, lsem.at[n])
        loads[name].start()

    loads["mw"].wait()
    wown[...] = mw_ref[...].astype(BF16)
    is_a = c == 0
    not_a = c == 1

    @pl.when(is_a)
    def _():
        wbuf[y, c] = wown[...]

    def dw_chunk(at):
        cols = pl.ds(pl.multiple_of(at * CH, 128), CH)
        return lax.dot_general(x_ref[:, cols], masked, (((0,), (0,)), ((), ())), preferred_element_type=F32)

    pl.semaphore_wait(barrier, len(near))

    s_wy = [sem("wy_up", 2), sem("wy_down", 2)]
    s_wsib = sem("wsib")
    for k in (0, 1):
        send(wown, wbuf.at[y, c], s_wy[k] + c, dev(yy=ys[k], cc=0))

    @pl.when(not_a)
    def _():
        send(wown, wbuf.at[y, c], s_wsib, dev(cc=sib))

    loads["hg"].wait()
    s_hg = sem("hg", 3)
    hgall[0, c] = hg_ref[...]
    send(hgall.at[0, c], hgall.at[1, c], s_hg, dev(xx=xp))
    send(hgall.at[0, c], hgall.at[0, c], s_hg + 1, dev(cc=sib))
    loads["cnt"].wait()

    row = lax.broadcasted_iota(I32, (ROWS, 32), 0)
    blk = lax.broadcasted_iota(I32, (ROWS, 32), 1)
    within = row - CAP * blk
    alive = (within >= 0) & (within < jnp.minimum(cnt_ref[...], CAP))
    alive = jnp.sum(jnp.where(alive, 1.0, 0.0), axis=1, keepdims=True) > 0.5
    masked = jnp.where(alive, hg_ref[...].astype(F32), 0.0).astype(BF16)

    b3 = lax.broadcasted_iota(I32, (8, BL, 1), 0)
    w3 = lax.broadcasted_iota(I32, (8, BL, 1), 1)
    r3 = jnp.where(w3 >= 40, 1, 0)
    v3 = w3 - 40 * r3
    l3 = jnp.where(v3 >= 20, 1, 0)
    u3 = v3 - 20 * l3
    c3 = jnp.where(u3 >= 10, 1, 0)
    p3 = u3 - 10 * c3
    z3 = (jnp.where(b3 < 4, z + sgn * b3, z - sgn * (b3 - 3)) + 16) & 7
    source = (r3 * ROWS + (l3 * 16 + z3 * 2 + c3) * CAP + p3).reshape(8 * BL, 1)
    perm = jnp.where(lax.broadcasted_iota(I32, (8 * BL, 2 * ROWS), 1) == source, 1.0, 0.0).astype(BF16)

    loads["x"].wait()
    part = SH // 2
    s_rx1 = [sem("rx1_right", 4), sem("rx1_left", 4)]
    s_rx2 = [sem("rx2_right", 4), sem("rx2_left", 4)]
    s_ry1 = [sem("ry1_up"), sem("ry1_down")]
    s_ry2 = [sem("ry2_up"), sem("ry2_down")]
    far_first = (2, 1, 3, 0)

    def yat(d):
        return (y + d) % 4

    sopp[...] = dw_chunk(x2).astype(BF16).reshape(4, 2, part, H)

    def grads_one():
        for d in far_first:
            for k in (0, 1):
                send(sopp.at[yat(d), k], rx1.at[k, yat(d)], s_rx1[k] + d, dev(xx=xs[k]))

    for k in (0, 1):
        sside[k] = dw_chunk(xs[k]).astype(BF16).reshape(4, 2, part, H)
    gown[...] = dw_chunk(x).reshape(4, SH, H)

    s_wyf = [sem("wyf_up"), sem("wyf_down")]
    s_wx = sem("wx", 4)
    order = (0, 3, 1, 2)

    def half_of(d, k):
        return wbuf.at[yat(d), :, pl.ds(k * part, part)]

    def spread(d):
        send(wbuf.at[yat(d)], wbuf.at[yat(d)], s_wx + d, dev(xx=xw, cc=sib))

    def gather_a():
        arrived(wbuf.at[y, sib], s_wsib)
        spread(0)
        for k, d in ((0, 3), (1, 1)):
            for s in (0, 1):
                arrived(wbuf.at[yat(d), s], s_wy[k] + s)
            send(half_of(d, k), half_of(d, k), s_wyf[k], dev(yy=ys[k]))
            spread(d)

    def gather_a_last():
        for k in (0, 1):
            arrived(half_of(2, k), s_wyf[k])
        spread(2)

    def gather_b():
        for d in (0, 3, 1):
            arrived(wbuf.at[yat(d)], s_wx + d)

    def gather_b_last():
        arrived(wbuf.at[y2], s_wx + 2)

    def rows_in():
        arrived(hgall.at[1, c], s_hg)
        send(hgall.at[1, c], hgall.at[1, c], s_hg + 2, dev(cc=sib))
        arrived(hgall.at[0, sib], s_hg + 1)
        arrived(hgall.at[1, sib], s_hg + 2)
        for s in (0, 1):
            both = jnp.concatenate([hgall[0, s], hgall[1, s]], axis=0)
            hgp[s] = jnp.dot(perm, both, preferred_element_type=F32).astype(BF16)

    n_units = len(UNITS)
    s_r1 = sem("rows1", n_units)
    s_r2 = sem("rows2", 4 * n_units)
    s_fin = sem("fin", 8 * n_units)

    def rows_one(u):
        total = jnp.zeros((8 * BL, WIDTHS[u]), F32)
        for s in (0, 1):
            weights = jnp.concatenate([wbuf[yat(d), s, pl.ds(at, n)] for d, at, n in UNITS[u]], axis=0)
            total += lax.dot_general(hgp[s], weights, (((1,), (1,)), ((), ())), preferred_element_type=F32)
        res[u][...] = total.astype(BF16).reshape(2, 4 * BL, WIDTHS[u])
        send(res[u].at[1], rcv1[u], s_r1 + u, dev(zz=(z - sgn + 8) % 8))

    def rows_two(u):
        arrived(rcv1[u], s_r1 + u)
        res[u][0] = (res[u][0].astype(F32) + rcv1[u][...].astype(F32)).astype(BF16)
        for t in (3, 2, 1):
            send(res[u].at[0, pl.ds(t * BL, BL)], rcv2[u].at[t], s_r2 + 4 * u + t, dev(zz=(z + sgn * t + 8) % 8))
        rcv2[u][0] = res[u][0, pl.ds(0, BL)]

    rr = lax.broadcasted_iota(I32, (256, 4 * BL), 0)
    col = lax.broadcasted_iota(I32, (1, 4 * BL), 1)
    tt = jnp.zeros_like(col)
    for t in (1, 2, 3):
        tt = tt + jnp.where(col >= t * BL, 1, 0)
    ww = col - BL * tt
    gg = jnp.zeros_like(col)
    for g in range(1, 8):
        gg = gg + jnp.where(ww >= g * CAP, 1, 0)
    expert = jnp.zeros_like(col)
    for t in range(4):
        step = -sgn * t if t % 2 == 0 else sgn * t
        expert = jnp.where(tt == t, ((z + step + 8) % 8) // 4, expert)
    target = gg * 32 + expert * CAP + ww - CAP * gg
    sorting = jnp.where(rr == target, 1.0, 0.0).astype(BF16)
    owners = [(rep, ll, cc) for rep in (1, 0) for ll in (1 - yl, yl) for cc in (c, sib)]

    def rows_three(u):
        for t in (1, 2, 3):
            arrived(rcv2[u].at[t], s_r2 + 4 * u + t)
        rows = jnp.dot(sorting, rcv2[u][...].reshape(4 * BL, WIDTHS[u]), preferred_element_type=F32)
        outg[u][...] = rows.astype(BF16).reshape(8, 32, WIDTHS[u])
        for k, (rep, ll, cc) in enumerate(owners):
            if k == 6:
                fin[u][0, c, yl] = outg[u][yl * 2 + c]
                continue
            send(outg[u].at[rep * 4 + ll * 2 + cc], fin[u].at[rep, c, yl], s_fin + 8 * u + k,
                 dev(xx=(x, xp)[rep], ll=ll, cc=cc), s_fin + 8 * u + 4 * rep + 2 * c + yl)

    def grads_two():
        for d in far_first:
            for k in (0, 1):
                arrived(rx1.at[k, yat(d)], s_rx1[k] + d)
                sside[k, yat(d), k] = (sside[k, yat(d), k].astype(F32) + rx1[k, yat(d)].astype(F32)).astype(BF16)
                send(sside.at[k, yat(d)], rx2.at[k, yat(d)], s_rx2[k] + d, dev(xx=xs[k]))

    def over_x(d):
        rows = gown[yat(d)]
        for k in (0, 1):
            arrived(rx2.at[k, yat(d)], s_rx2[k] + d)
            rows = rows + rx2[k, yat(d)].reshape(SH, H).astype(F32)
        return rows

    def grads_three():
        ysopp[...] = over_x(2).astype(BF16).reshape(2, part, H)
        for k in (0, 1):
            send(ysopp.at[k], ry1.at[k], s_ry1[k], dev(yy=ys[k]))

    def grads_four():
        for k, d in ((0, 1), (1, 3)):
            rows = over_x(d).reshape(2, part, H)
            arrived(ry1.at[k], s_ry1[k])
            ysside[k, k] = (rows[k] + ry1[k].astype(F32)).astype(BF16)
            ysside[k, 1 - k] = rows[1 - k].astype(BF16)
            send(ysside.at[k], ry2.at[k], s_ry2[k], dev(yy=ys[k]))

    def adam():
        grads = over_x(0)
        for k in (0, 1):
            arrived(ry2.at[k], s_ry2[k])
        for name in ("m1", "m2"):
            loads[name].wait()
        grads = grads + ry2[0].reshape(SH, H).astype(F32) + ry2[1].reshape(SH, H).astype(F32)
        master = mw_ref[...]
        new_first = beta_one * m1_ref[...] + (1.0 - beta_one) * grads
        new_second = beta_two * m2_ref[...] + (1.0 - beta_two) * grads * grads
        first_hat = new_first / (1.0 - beta_one**step_count)
        second_hat = new_second / (1.0 - beta_two**step_count)
        nw_ref[...] = master - learn_rate * (
            first_hat / (jnp.sqrt(second_hat) + adam_epsilon) + weight_decay * master
        )
        n1_ref[...] = new_first
        n2_ref[...] = new_second

    from_col = lax.broadcasted_iota(I32, (CH, 1), 0)
    belongs = jnp.zeros_like(from_col)
    done = 0
    for unit in UNITS:
        for d, at, n in unit:
            belongs = jnp.where(from_col >= done, yat(d) * SH + at + from_col - done, belongs)
            done += n
    place[...] = jnp.where(lax.broadcasted_iota(I32, (CH, CH), 1) == belongs, 1.0, 0.0).astype(BF16)

    @pl.when(is_a)
    def _():
        gather_a()
        grads_one()
        rows_in()
        rows_one(0)
        gather_a_last()
        rows_one(1)
        grads_two()
        rows_two(0)

    @pl.when(not_a)
    def _():
        grads_one()
        rows_in()
        gather_b()
        rows_one(0)
        grads_two()
        gather_b_last()
        rows_one(1)
        rows_two(0)

    rows_two(1)
    grads_three()
    rows_three(0)
    grads_four()
    rows_three(1)
    adam()

    wanted = lax.broadcasted_iota(I32, (64, 128), 0)
    table = jnp.zeros((64, 128), F32)
    loads["ids"].wait()
    loads["slots"].wait()
    for r in range(ids_ref.shape[0]):
        expert_id = ids_ref[pl.ds(r, 1), :]
        slot_id = slots_ref[pl.ds(r, 1), :]
        lower = jnp.where(expert_id >= 2, 1, 0)
        code = lower * 32 + (expert_id - 2 * lower) * CAP + slot_id
        code = jnp.where((slot_id >= 0) & (expert_id < 4), code, -1)
        table = table + jnp.where(wanted == code, 1.0, 0.0)
    table = table.astype(BF16)

    for u in range(n_units):
        for rep in (0, 1):
            for ll in (yl, 1 - yl):
                for cc in (c, sib):
                    if rep == 1 or ll is not yl or cc is not c:
                        arrived(fin[u].at[rep, cc, ll], s_fin + 8 * u + 4 * rep + 2 * cc + ll)
    for rep in (0, 1):
        for cc in (0, 1):
            natural = jnp.zeros((64, CH), F32)
            for u in range(n_units):
                natural += jnp.dot(
                    fin[u][rep, cc].reshape(64, WIDTHS[u]), place[pl.ds(PLACES[u], WIDTHS[u])],
                    preferred_element_type=F32,
                )
            from_x = (x, xp)[rep]
            chunk = (from_x, 3 - from_x)[cc]
            out_ref[:, pl.ds(pl.multiple_of(chunk * CH, 128), CH)] = lax.dot_general(
                table, natural.astype(BF16), (((0,), (0,)), ((), ())), preferred_element_type=F32
            ).astype(BF16)

    for k in (0, 1):
        sent(wown, s_wy[k] + c)
        for d in order:
            sent(sopp.at[yat(d), k], s_rx1[k] + d)
            sent(sside.at[k, yat(d)], s_rx2[k] + d)
        sent(ysopp.at[k], s_ry1[k])
        sent(ysside.at[k], s_ry2[k])
    for u in range(n_units):
        sent(res[u].at[1], s_r1 + u)
        for t in (1, 2, 3):
            sent(res[u].at[0, pl.ds(t * BL, BL)], s_r2 + 4 * u + t)
        for k in (0, 1, 2, 3, 4, 5, 7):
            sent(outg[u].at[k], s_fin + 8 * u + k)
    for k in (0, 1):
        sent(hgall.at[0, c], s_hg + k)
    sent(hgall.at[1, c], s_hg + 2)

    @pl.when(is_a)
    def _():
        for k, d in ((0, 3), (1, 1)):
            sent(half_of(d, k), s_wyf[k])
        for d in order:
            sent(wbuf.at[yat(d)], s_wx + d)

    @pl.when(not_a)
    def _():
        sent(wown, s_wsib)


def body(expert_inputs, hidden_grads, row_counts, top_ids, route_slots, master, first, second):
    vmem = pl.BlockSpec(memory_space=pltpu.VMEM)
    shard = jax.ShapeDtypeStruct((SH, H), F32)
    out, new_master, new_first, new_second = pl.pallas_call(
        kernel,
        out_shape=(jax.ShapeDtypeStruct((128, D), BF16), shard, shard, shard),
        in_specs=[pl.BlockSpec(memory_space=pltpu.HBM)] * 8,
        out_specs=(vmem,) * 4,
        scratch_shapes=[
            pltpu.VMEM((ROWS, D), BF16),
            pltpu.VMEM((ROWS, H), BF16),
            pltpu.VMEM((1, 32), I32),
            pltpu.VMEM((8, 128), I32),
            pltpu.VMEM((8, 128), I32),
            pltpu.VMEM((SH, H), F32),
            pltpu.VMEM((SH, H), F32),
            pltpu.VMEM((SH, H), F32),
            pltpu.VMEM((SH, H), BF16),
            pltpu.VMEM((4, 2, SH, H), BF16),
            pltpu.VMEM((2, 2, ROWS, H), BF16),
            pltpu.VMEM((2, 8 * BL, H), BF16),
            pltpu.VMEM((CH, CH), BF16),
            pltpu.VMEM((4, 2, SH // 2, H), BF16),
            pltpu.VMEM((2, 4, 2, SH // 2, H), BF16),
            pltpu.VMEM((2, 4, SH // 2, H), BF16),
            pltpu.VMEM((2, 4, 2, SH // 2, H), BF16),
            pltpu.VMEM((2, SH // 2, H), BF16),
            pltpu.VMEM((2, 2, SH // 2, H), BF16),
            pltpu.VMEM((2, SH // 2, H), BF16),
            pltpu.VMEM((2, 2, SH // 2, H), BF16),
            pltpu.VMEM((4, SH, H), F32),
            pltpu.SemaphoreType.DMA((N_SEM,)),
            pltpu.SemaphoreType.DMA((N_SEM,)),
            pltpu.SemaphoreType.DMA((8,)),
            *[pltpu.VMEM((2, 4 * BL, n), BF16) for n in WIDTHS],
            *[pltpu.VMEM((4 * BL, n), BF16) for n in WIDTHS],
            *[pltpu.VMEM((4, BL, n), BF16) for n in WIDTHS],
            *[pltpu.VMEM((8, 32, n), BF16) for n in WIDTHS],
            *[pltpu.VMEM((2, 2, 2, 32, n), BF16) for n in WIDTHS],
        ],
        compiler_params=pltpu.CompilerParams(
            collective_id=0, has_side_effects=True, vmem_limit_bytes=56 * 2**20
        ),
    )(
        expert_inputs, hidden_grads, row_counts.reshape(1, 32), top_ids.T, route_slots.T,
        master[0], first[0], second[0],
    )
    return out, new_master[None], new_first[None], new_second[None]


def solution(mesh):
    rows = P(("dp", "ep"), None)
    weights = P("ep", "dp", None)
    return jax.shard_map(
        body,
        mesh=mesh,
        in_specs=(rows, rows, P(("dp", "ep")), rows, rows, weights, weights, weights),
        out_specs=(rows, weights, weights, weights),
        check_vma=False,
    )
```

```python
import jax
import jax.numpy as jnp
from jax import lax
from jax.experimental import pallas as pl
from jax.experimental.pallas import tpu as pltpu
from jax.sharding import PartitionSpec as P

MESH = pl.DeviceIdType.MESH
F32 = jnp.float32
BF16 = jnp.bfloat16
I32 = jnp.int32

beta_one = 0.9
beta_two = 0.999
learn_rate = 0.001
adam_epsilon = 1e-08
weight_decay = 0.1
step_count = 100

D = 3584
H = 256
SH = 224
PART = 112
CH = 896
CAP = 10
ROWS = 320
BL = 80
N_SEM = 128
UNITS = (((0, 0, 112), (1, 0, 112), (3, 0, 32)), ((3, 32, 80), (2, 0, 112)))
FILL = (0, 64)
WIDTHS = tuple(sum(n for _, _, n in unit) + fill for unit, fill in zip(UNITS, FILL))
PLACES = tuple(sum(WIDTHS[:u]) for u in range(len(WIDTHS)))


def kernel(
    x_hbm, hg_hbm, cnt_hbm, ids_hbm, slots_hbm, mw_hbm, m1_hbm, m2_hbm,
    out_hbm, nw_hbm, n1_hbm, n2_hbm,
    out_ref, nw_ref, n1_ref, n2_ref,
    x_ref, hg_ref, cnt_ref, ids_ref, slots_ref, mw_ref, m1_ref, m2_ref,
    wown, wz, wbuf, hgall, hgp, place, sopp, sside, rx1, rx2, ysopp, ysside, ry1, ry2, gown,
    ssem, rsem, lsem, *by_unit,
):
    n_units = len(UNITS)
    res, rcv, outg, fin = (by_unit[n_units * n : n_units * (n + 1)] for n in range(4))

    dp = lax.axis_index("dp")
    ep = lax.axis_index("ep")
    x, y = dp // 4, dp % 4
    yl, z, c = ep // 16, (ep // 2) % 8, ep % 2
    b = z % 2
    zq = z + 1 - 2 * b
    sib = 1 - c
    xs = ((x + 1) % 4, (x + 3) % 4)
    ys = ((y + 1) % 4, (y + 3) % 4)
    x2, y2 = (x + 2) % 4, (y + 2) % 4
    xp = x + 1 - 2 * (x % 2)
    xw = 3 - x

    def dev(xx=None, yy=None, ll=None, zz=None, cc=None):
        xx = x if xx is None else xx
        yy = y if yy is None else yy
        ll = yl if ll is None else ll
        zz = z if zz is None else zz
        cc = c if cc is None else cc
        return {"dp": xx * 4 + yy, "ep": ll * 16 + zz * 2 + cc}

    spots = {}
    used = [0]

    def sem(name, many=1):
        if name not in spots:
            spots[name] = used[0]
            used[0] += many
        return spots[name]

    def copy(src, dst, at, to, landing=None):
        return pltpu.make_async_remote_copy(
            src_ref=src, dst_ref=dst, send_sem=ssem.at[at], recv_sem=rsem.at[at if landing is None else landing],
            device_id=to, device_id_type=MESH,
        )

    def arrived(dst, at):
        copy(dst, dst, at, dev(cc=sib)).wait_recv()

    def sent(src, at):
        copy(src, src, at, dev(cc=sib)).wait_send()

    def send(src, dst, at, to, landing=None):
        copy(src, dst, at, to, landing).start()

    barrier = pltpu.get_barrier_semaphore()
    near = [dev(cc=sib), dev(xx=xs[0]), dev(xx=xs[1])]
    near += [dev(yy=yy, cc=cc) for yy in ys for cc in (c, sib)]
    near += [dev(zz=(z + t) % 8) for t in range(1, 8)]
    near += [dev(xx=xp, cc=sib), dev(xx=xw, cc=sib)]
    near += [dev(xx=xx, ll=1 - yl, cc=cc) for xx in (x, xp) for cc in (c, sib)]
    for to in near:
        pl.semaphore_signal(barrier, inc=1, device_id=to, device_id_type=MESH)

    loads = {}
    pairs = (
        ("mw", mw_hbm, mw_ref), ("hg", hg_hbm, hg_ref), ("cnt", cnt_hbm, cnt_ref), ("x", x_hbm, x_ref),
        ("ids", ids_hbm, ids_ref), ("slots", slots_hbm, slots_ref), ("m1", m1_hbm, m1_ref), ("m2", m2_hbm, m2_ref),
    )
    for n, (name, there, here) in enumerate(pairs):
        loads[name] = pltpu.make_async_copy(there, here, lsem.at[n])
        loads[name].start()

    loads["mw"].wait()
    wown[...] = mw_ref[...].astype(BF16).reshape(2, PART, H)
    is_a = c == 0
    not_a = c == 1

    @pl.when(is_a)
    def _():
        wbuf[y, 0, c] = wown[b]

    def dw_chunk(at):
        cols = pl.ds(pl.multiple_of(at * CH, 128), CH)
        return lax.dot_general(x_ref[:, cols], masked, (((0,), (0,)), ((), ())), preferred_element_type=F32)

    pl.semaphore_wait(barrier, len(near))

    s_wz = sem("wz")
    s_wy = [sem("wy_up", 4), sem("wy_down", 4)]
    s_wsib = sem("wsib", 2)
    send(wown.at[1 - b], wz, s_wz, dev(zz=zq))

    def to_y(rel, here):
        for k in (0, 1):
            send(here, wbuf.at[y, rel, c], s_wy[k] + 2 * rel + c, dev(yy=ys[k], cc=0))

        @pl.when(not_a)
        def _():
            send(here, wbuf.at[y, rel, c], s_wsib + rel, dev(cc=sib))

    to_y(0, wown.at[b])

    loads["hg"].wait()
    s_hg = sem("hg", 7)
    hgall[0, 0, c] = hg_ref[...]
    send(hgall.at[0, 0, c], hgall.at[1, 0, c], s_hg + 2, dev(xx=xp))
    send(hgall.at[0, 0, c], hgall.at[0, 1, c], s_hg + 1, dev(zz=zq))
    send(hgall.at[0, 0, c], hgall.at[0, 0, c], s_hg, dev(cc=sib))
    loads["cnt"].wait()

    row = lax.broadcasted_iota(I32, (ROWS, 32), 0)
    blk = lax.broadcasted_iota(I32, (ROWS, 32), 1)
    within = row - CAP * blk
    alive = (within >= 0) & (within < jnp.minimum(cnt_ref[...], CAP))
    alive = jnp.sum(jnp.where(alive, 1.0, 0.0), axis=1, keepdims=True) > 0.5
    masked = jnp.where(alive, hg_ref[...].astype(F32), 0.0).astype(BF16)

    b3 = lax.broadcasted_iota(I32, (8, BL, 1), 0)
    w3 = lax.broadcasted_iota(I32, (8, BL, 1), 1)
    r3 = jnp.where(w3 >= 40, 1, 0)
    v3 = w3 - 40 * r3
    l3 = jnp.where(v3 >= 20, 1, 0)
    u3 = v3 - 20 * l3
    c3 = jnp.where(u3 >= 10, 1, 0)
    p3 = u3 - 10 * c3
    z3 = (z + b3) & 7
    source = (r3 * ROWS + (l3 * 16 + z3 * 2 + c3) * CAP + p3).reshape(8 * BL, 1)
    perm = jnp.where(lax.broadcasted_iota(I32, (8 * BL, 2 * ROWS), 1) == source, 1.0, 0.0).astype(BF16)

    loads["x"].wait()
    part = SH // 2
    s_rx1 = [sem("rx1_right", 4), sem("rx1_left", 4)]
    s_rx2 = [sem("rx2_right", 4), sem("rx2_left", 4)]
    s_ry1 = [sem("ry1_up"), sem("ry1_down")]
    s_ry2 = [sem("ry2_up"), sem("ry2_down")]
    far_first = (2, 1, 3, 0)

    def yat(d):
        return (y + d) % 4

    sopp[...] = dw_chunk(x2).astype(BF16).reshape(4, 2, part, H)

    def grads_one():
        for d in far_first:
            for k in (0, 1):
                send(sopp.at[yat(d), k], rx1.at[k, yat(d)], s_rx1[k] + d, dev(xx=xs[k]))

    for k in (0, 1):
        sside[k] = dw_chunk(xs[k]).astype(BF16).reshape(4, 2, part, H)
    gown[...] = dw_chunk(x).reshape(4, SH, H)

    arrived(wz, s_wz)
    to_y(1, wz)

    @pl.when(is_a)
    def _():
        wbuf[y, 1, c] = wz[...]

    s_wyf = [sem("wyf_up"), sem("wyf_down")]
    s_wx = sem("wx", 4)
    order = (0, 3, 1, 2)

    def half_of(d, k):
        return wbuf.at[yat(d), k]

    def spread(d):
        send(wbuf.at[yat(d)], wbuf.at[yat(d)], s_wx + d, dev(xx=xw, cc=sib))

    def gather_a_first():
        for rel in (0, 1):
            arrived(wbuf.at[y, rel, sib], s_wsib + rel)
        spread(0)

    def gather_a():
        for k, d in ((0, 3), (1, 1)):
            for rel in (0, 1):
                for cc in (0, 1):
                    arrived(wbuf.at[yat(d), rel, cc], s_wy[k] + 2 * rel + cc)
                if rel == k:
                    send(half_of(d, k), half_of(d, k), s_wyf[k], dev(yy=ys[k]))
            spread(d)

    def gather_a_last():
        for k in (0, 1):
            arrived(half_of(2, k), s_wyf[k])
        spread(2)

    def gather_b():
        for d in (0, 3, 1):
            arrived(wbuf.at[yat(d)], s_wx + d)

    def gather_b_last():
        arrived(wbuf.at[y2], s_wx + 2)

    def pass_on():
        arrived(hgall.at[1, 0, c], s_hg + 2)
        send(hgall.at[1, 0, c], hgall.at[1, 1, c], s_hg + 4, dev(zz=zq))
        send(hgall.at[1, 0, c], hgall.at[1, 0, c], s_hg + 3, dev(cc=sib))
        arrived(hgall.at[0, 1, c], s_hg + 1)
        send(hgall.at[0, 1, c], hgall.at[0, 1, c], s_hg + 5, dev(cc=sib))

    def rows_in():
        arrived(hgall.at[1, 1, c], s_hg + 4)
        send(hgall.at[1, 1, c], hgall.at[1, 1, c], s_hg + 6, dev(cc=sib))
        arrived(hgall.at[0, 0, sib], s_hg)
        arrived(hgall.at[1, 0, sib], s_hg + 3)
        arrived(hgall.at[0, 1, sib], s_hg + 5)
        arrived(hgall.at[1, 1, sib], s_hg + 6)
        for rel in (0, 1):
            for cc in (0, 1):
                both = jnp.concatenate([hgall[0, rel, cc], hgall[1, rel, cc]], axis=0)
                hgp[rel, cc] = jnp.dot(perm, both, preferred_element_type=F32).astype(BF16)

    s_rows = sem("rows", 8 * n_units)
    s_fin = sem("fin", 8 * n_units)
    far = (4, 3, 5, 2, 6, 1, 7)

    def rows_one(u):
        total = jnp.zeros((8 * BL, WIDTHS[u]), F32)
        for rel in (0, 1):
            for cc in (0, 1):
                pieces = [wbuf[yat(d), rel, cc, pl.ds(at, n)] for d, at, n in UNITS[u]]
                if FILL[u]:
                    pieces.append(wbuf[y, rel, cc, pl.ds(0, FILL[u])])
                weights = jnp.concatenate(pieces, axis=0)
                total += lax.dot_general(hgp[rel, cc], weights, (((1,), (1,)), ((), ())), preferred_element_type=F32)
        res[u][...] = total.astype(BF16).reshape(8, BL, WIDTHS[u])
        for i in far:
            send(res[u].at[i], rcv[u].at[i % 2, i // 2], s_rows + 8 * u + i, dev(zz=(z + i) % 8))
        rcv[u][0, 0] = res[u][0]

    rr = lax.broadcasted_iota(I32, (256, 4 * BL), 0)
    col = lax.broadcasted_iota(I32, (1, 4 * BL), 1)
    tt = jnp.zeros_like(col)
    for t in (1, 2, 3):
        tt = tt + jnp.where(col >= t * BL, 1, 0)
    ww = col - BL * tt
    gg = jnp.zeros_like(col)
    for g in range(1, 8):
        gg = gg + jnp.where(ww >= g * CAP, 1, 0)

    def sorting(par):
        expert = jnp.where(((z + 16 - 2 * tt - par) & 7) >= 4, 1, 0)
        target = gg * 32 + expert * CAP + ww - CAP * gg
        return jnp.where(rr == target, 1.0, 0.0).astype(BF16)

    owners = [(rep, ll, cc) for rep in (1, 0) for ll in (1 - yl, yl) for cc in (c, sib)]

    def rows_two(u):
        for par in (0, 1):
            for t in range(4):
                i = 2 * t + par
                if i:
                    arrived(rcv[u].at[par, t], s_rows + 8 * u + i)
            rows = jnp.dot(sorting(par), rcv[u][par].reshape(4 * BL, WIDTHS[u]), preferred_element_type=F32)
            outg[u][:, par] = rows.astype(BF16).reshape(8, 32, WIDTHS[u])
        for k, (rep, ll, cc) in enumerate(owners):
            if k == 6:
                fin[u][0, c, yl] = outg[u][yl * 2 + c]
                continue
            send(outg[u].at[rep * 4 + ll * 2 + cc], fin[u].at[rep, c, yl], s_fin + 8 * u + k,
                 dev(xx=(x, xp)[rep], ll=ll, cc=cc), s_fin + 8 * u + 4 * rep + 2 * c + yl)

    def grads_two():
        for d in far_first:
            for k in (0, 1):
                arrived(rx1.at[k, yat(d)], s_rx1[k] + d)
                sside[k, yat(d), k] = (sside[k, yat(d), k].astype(F32) + rx1[k, yat(d)].astype(F32)).astype(BF16)
                send(sside.at[k, yat(d)], rx2.at[k, yat(d)], s_rx2[k] + d, dev(xx=xs[k]))

    def over_x(d):
        rows = gown[yat(d)]
        for k in (0, 1):
            arrived(rx2.at[k, yat(d)], s_rx2[k] + d)
            rows = rows + rx2[k, yat(d)].reshape(SH, H).astype(F32)
        return rows

    def grads_three():
        ysopp[...] = over_x(2).astype(BF16).reshape(2, part, H)
        for k in (0, 1):
            send(ysopp.at[k], ry1.at[k], s_ry1[k], dev(yy=ys[k]))

    def grads_four():
        for k, d in ((0, 1), (1, 3)):
            rows = over_x(d).reshape(2, part, H)
            arrived(ry1.at[k], s_ry1[k])
            ysside[k, k] = (rows[k] + ry1[k].astype(F32)).astype(BF16)
            ysside[k, 1 - k] = rows[1 - k].astype(BF16)
            send(ysside.at[k], ry2.at[k], s_ry2[k], dev(yy=ys[k]))

    leaves = []

    def adam():
        grads = over_x(0)
        for k in (0, 1):
            arrived(ry2.at[k], s_ry2[k])
        for name in ("m1", "m2"):
            loads[name].wait()
        grads = grads + ry2[0].reshape(SH, H).astype(F32) + ry2[1].reshape(SH, H).astype(F32)
        master = mw_ref[...]
        new_first = beta_one * m1_ref[...] + (1.0 - beta_one) * grads
        new_second = beta_two * m2_ref[...] + (1.0 - beta_two) * grads * grads
        first_hat = new_first / (1.0 - beta_one**step_count)
        second_hat = new_second / (1.0 - beta_two**step_count)
        nw_ref[...] = master - learn_rate * (
            first_hat / (jnp.sqrt(second_hat) + adam_epsilon) + weight_decay * master
        )
        n1_ref[...] = new_first
        n2_ref[...] = new_second
        for n, (here, there) in enumerate(((nw_ref, nw_hbm), (n1_ref, n1_hbm), (n2_ref, n2_hbm))):
            leaves.append(pltpu.make_async_copy(here, there, lsem.at[8 + n]))
            leaves[-1].start()

    from_col = lax.broadcasted_iota(I32, (PLACES[-1] + WIDTHS[-1], 1), 0)
    belongs = jnp.zeros_like(from_col)
    for u in range(n_units):
        done = PLACES[u]
        for d, at, n in UNITS[u]:
            belongs = jnp.where(from_col >= done, yat(d) * SH + at + from_col - done, belongs)
            done += n
        if FILL[u]:
            belongs = jnp.where(from_col >= done, -SH, belongs)
    to_col = lax.broadcasted_iota(I32, (PLACES[-1] + WIDTHS[-1], CH), 1)
    for par in (0, 1):
        rows_of = b if par == 0 else 1 - b
        place[par] = jnp.where(to_col == belongs + rows_of * PART, 1.0, 0.0).astype(BF16)

    @pl.when(is_a)
    def _():
        gather_a_first()
        grads_one()
        pass_on()
        gather_a()
        rows_in()
        rows_one(0)
        gather_a_last()
        rows_one(1)
        grads_two()

    @pl.when(not_a)
    def _():
        grads_one()
        pass_on()
        rows_in()
        gather_b()
        rows_one(0)
        grads_two()
        gather_b_last()
        rows_one(1)

    grads_three()
    rows_two(0)
    grads_four()
    rows_two(1)
    adam()

    wanted = lax.broadcasted_iota(I32, (64, 128), 0)
    table = jnp.zeros((64, 128), F32)
    loads["ids"].wait()
    loads["slots"].wait()
    for r in range(ids_ref.shape[0]):
        expert_id = ids_ref[pl.ds(r, 1), :]
        slot_id = slots_ref[pl.ds(r, 1), :]
        lower = jnp.where(expert_id >= 2, 1, 0)
        code = lower * 32 + (expert_id - 2 * lower) * CAP + slot_id
        code = jnp.where((slot_id >= 0) & (expert_id < 4), code, -1)
        table = table + jnp.where(wanted == code, 1.0, 0.0)
    table = table.astype(BF16)

    for u in range(n_units):
        for rep in (0, 1):
            for ll in (yl, 1 - yl):
                for cc in (c, sib):
                    if rep == 1 or ll is not yl or cc is not c:
                        arrived(fin[u].at[rep, cc, ll], s_fin + 8 * u + 4 * rep + 2 * cc + ll)
    for rep in (0, 1):
        for cc in (0, 1):
            natural = jnp.zeros((64, CH), F32)
            for u in range(n_units):
                for par in (0, 1):
                    natural += jnp.dot(
                        fin[u][rep, cc, :, par].reshape(64, WIDTHS[u]), place[par, pl.ds(PLACES[u], WIDTHS[u])],
                        preferred_element_type=F32,
                    )
            from_x = (x, xp)[rep]
            chunk = (from_x, 3 - from_x)[cc]
            out_ref[rep, cc] = lax.dot_general(
                table, natural.astype(BF16), (((0,), (0,)), ((), ())), preferred_element_type=F32
            ).astype(BF16)
            there = out_hbm.at[:, pl.ds(pl.multiple_of(chunk * CH, 128), CH)]
            leaves.append(pltpu.make_async_copy(out_ref.at[rep, cc], there, lsem.at[11 + 2 * rep + cc]))
            leaves[-1].start()

    for leaf in leaves:
        leaf.wait()
    for k in (0, 1):
        for rel in (0, 1):
            sent(wz, s_wy[k] + 2 * rel + c)
        for d in order:
            sent(sopp.at[yat(d), k], s_rx1[k] + d)
            sent(sside.at[k, yat(d)], s_rx2[k] + d)
        sent(ysopp.at[k], s_ry1[k])
        sent(ysside.at[k], s_ry2[k])
    sent(wz, s_wz)
    for u in range(n_units):
        for i in far:
            sent(res[u].at[i], s_rows + 8 * u + i)
        for k in (0, 1, 2, 3, 4, 5, 7):
            sent(outg[u].at[k], s_fin + 8 * u + k)
    for k in range(7):
        sent(hgall.at[0, 0, c], s_hg + k)

    @pl.when(is_a)
    def _():
        for k, d in ((0, 3), (1, 1)):
            sent(half_of(d, k), s_wyf[k])
        for d in order:
            sent(wbuf.at[yat(d)], s_wx + d)

    @pl.when(not_a)
    def _():
        for rel in (0, 1):
            sent(wz, s_wsib + rel)


def hand_over(*refs):
    there, held, back, sems = refs[:4], refs[8:12], refs[4:8], refs[12]
    loads = [pltpu.make_async_copy(there[n], held[n], sems.at[n]) for n in range(4)]
    stores = [pltpu.make_async_copy(held[n], back[n], sems.at[4 + n]) for n in range(4)]
    for load in loads:
        load.start()
    for load, store in zip(loads, stores):
        load.wait()
        store.start()
    for store in stores:
        store.wait()


def body(expert_inputs, hidden_grads, row_counts, top_ids, route_slots, master, first, second):
    hbm = pl.BlockSpec(memory_space=pltpu.HBM)
    shard = jax.ShapeDtypeStruct((SH, H), F32)
    results = pl.pallas_call(
        kernel,
        out_shape=(jax.ShapeDtypeStruct((128, D), BF16), shard, shard, shard),
        in_specs=[hbm] * 8,
        out_specs=(hbm,) * 4,
        scratch_shapes=[
            pltpu.VMEM((2, 2, 128, CH), BF16),
            pltpu.VMEM((SH, H), F32),
            pltpu.VMEM((SH, H), F32),
            pltpu.VMEM((SH, H), F32),
            pltpu.VMEM((ROWS, D), BF16),
            pltpu.VMEM((ROWS, H), BF16),
            pltpu.VMEM((1, 32), I32),
            pltpu.VMEM((8, 128), I32),
            pltpu.VMEM((8, 128), I32),
            pltpu.VMEM((SH, H), F32),
            pltpu.VMEM((SH, H), F32),
            pltpu.VMEM((SH, H), F32),
            pltpu.VMEM((2, PART, H), BF16),
            pltpu.VMEM((PART, H), BF16),
            pltpu.VMEM((4, 2, 2, PART, H), BF16),
            pltpu.VMEM((2, 2, 2, ROWS, H), BF16),
            pltpu.VMEM((2, 2, 8 * BL, H), BF16),
            pltpu.VMEM((2, PLACES[-1] + WIDTHS[-1], CH), BF16),
            pltpu.VMEM((4, 2, SH // 2, H), BF16),
            pltpu.VMEM((2, 4, 2, SH // 2, H), BF16),
            pltpu.VMEM((2, 4, SH // 2, H), BF16),
            pltpu.VMEM((2, 4, 2, SH // 2, H), BF16),
            pltpu.VMEM((2, SH // 2, H), BF16),
            pltpu.VMEM((2, 2, SH // 2, H), BF16),
            pltpu.VMEM((2, SH // 2, H), BF16),
            pltpu.VMEM((2, 2, SH // 2, H), BF16),
            pltpu.VMEM((4, SH, H), F32),
            pltpu.SemaphoreType.DMA((N_SEM,)),
            pltpu.SemaphoreType.DMA((N_SEM,)),
            pltpu.SemaphoreType.DMA((16,)),
            *[pltpu.VMEM((8, BL, n), BF16) for n in WIDTHS],
            *[pltpu.VMEM((2, 4, BL, n), BF16) for n in WIDTHS],
            *[pltpu.VMEM((8, 2, 32, n), BF16) for n in WIDTHS],
            *[pltpu.VMEM((2, 2, 2, 2, 32, n), BF16) for n in WIDTHS],
        ],
        compiler_params=pltpu.CompilerParams(
            collective_id=0, has_side_effects=True, vmem_limit_bytes=56 * 2**20
        ),
    )(
        expert_inputs, hidden_grads, row_counts.reshape(1, 32), top_ids.T, route_slots.T,
        master[0], first[0], second[0],
    )
    out, new_master, new_first, new_second = pl.pallas_call(
        hand_over,
        out_shape=(jax.ShapeDtypeStruct((128, D), BF16), shard, shard, shard),
        in_specs=[hbm] * 4,
        out_specs=(hbm,) * 4,
        scratch_shapes=[
            pltpu.VMEM((128, D), BF16),
            *[pltpu.VMEM((SH, H), F32)] * 3,
            pltpu.SemaphoreType.DMA((8,)),
        ],
        compiler_params=pltpu.CompilerParams(vmem_limit_bytes=56 * 2**20),
    )(*results)
    return out, new_master[None], new_first[None], new_second[None]


def solution(mesh):
    rows = P(("dp", "ep"), None)
    weights = P("ep", "dp", None)
    return jax.shard_map(
        body,
        mesh=mesh,
        in_specs=(rows, rows, P(("dp", "ep")), rows, rows, weights, weights, weights),
        out_specs=(rows, weights, weights, weights),
        check_vma=False,
    )
```

```python
import jax
import jax.numpy as jnp
from jax import lax
from jax.experimental import pallas as pl
from jax.experimental.pallas import tpu as pltpu
from jax.sharding import PartitionSpec as P

MESH = pl.DeviceIdType.MESH
F32 = jnp.float32
BF16 = jnp.bfloat16
I32 = jnp.int32

beta_one = 0.9
beta_two = 0.999
learn_rate = 0.001
adam_epsilon = 1e-08
weight_decay = 0.1
step_count = 100

D = 3584
H = 256
SH = 224
PART = 112
CH = 896
CAP = 10
ROWS = 320
BL = 80
N_SEM = 128
UNITS = (((0, 0, 112), (1, 0, 112), (3, 0, 32)), ((3, 32, 80), (2, 0, 112)))
WIDTHS = tuple(sum(n for _, _, n in unit) for unit in UNITS)
PLACES = tuple(sum(WIDTHS[:u]) for u in range(len(WIDTHS)))


def kernel(
    x_hbm, hg_hbm, cnt_hbm, ids_hbm, slots_hbm, mw_hbm, m1_hbm, m2_hbm,
    out_hbm, nw_hbm, n1_hbm, n2_hbm,
    out_ref, nw_ref, n1_ref, n2_ref,
    x_ref, hg_ref, cnt_ref, ids_ref, slots_ref, mw_ref, m1_ref, m2_ref,
    wown, wz, wbuf, hgall, hgp, place, sopp, sside, rx1, rx2, ysopp, ysside, ry1, ry2, gown,
    ssem, rsem, lsem, *by_unit,
):
    n_units = len(UNITS)
    res, rcv, outg, fin = (by_unit[n_units * n : n_units * (n + 1)] for n in range(4))

    dp = lax.axis_index("dp")
    ep = lax.axis_index("ep")
    x, y = dp // 4, dp % 4
    yl, z, c = ep // 16, (ep // 2) % 8, ep % 2
    b = z % 2
    zq = z + 1 - 2 * b
    sib = 1 - c
    xs = ((x + 1) % 4, (x + 3) % 4)
    ys = ((y + 1) % 4, (y + 3) % 4)
    x2, y2 = (x + 2) % 4, (y + 2) % 4
    xp = x + 1 - 2 * (x % 2)
    xw = 3 - x

    def dev(xx=None, yy=None, ll=None, zz=None, cc=None):
        xx = x if xx is None else xx
        yy = y if yy is None else yy
        ll = yl if ll is None else ll
        zz = z if zz is None else zz
        cc = c if cc is None else cc
        return {"dp": xx * 4 + yy, "ep": ll * 16 + zz * 2 + cc}

    spots = {}
    used = [0]

    def sem(name, many=1):
        if name not in spots:
            spots[name] = used[0]
            used[0] += many
        return spots[name]

    def copy(src, dst, at, to, landing=None):
        return pltpu.make_async_remote_copy(
            src_ref=src, dst_ref=dst, send_sem=ssem.at[at], recv_sem=rsem.at[at if landing is None else landing],
            device_id=to, device_id_type=MESH,
        )

    def arrived(dst, at):
        copy(dst, dst, at, dev(cc=sib)).wait_recv()

    def sent(src, at):
        copy(src, src, at, dev(cc=sib)).wait_send()

    def send(src, dst, at, to, landing=None):
        copy(src, dst, at, to, landing).start()

    barrier = pltpu.get_barrier_semaphore()
    near = [dev(cc=sib), dev(xx=xs[0]), dev(xx=xs[1])]
    near += [dev(yy=yy, cc=cc) for yy in ys for cc in (c, sib)]
    near += [dev(zz=(z + t) % 8) for t in range(1, 8)]
    near += [dev(xx=xp, cc=sib), dev(xx=xw, cc=sib)]
    near += [dev(xx=xx, ll=1 - yl, cc=cc) for xx in (x, xp) for cc in (c, sib)]
    for to in near:
        pl.semaphore_signal(barrier, inc=1, device_id=to, device_id_type=MESH)

    loads = {}
    pairs = (
        ("mw", mw_hbm, mw_ref), ("hg", hg_hbm, hg_ref), ("cnt", cnt_hbm, cnt_ref), ("x", x_hbm, x_ref),
        ("ids", ids_hbm, ids_ref), ("slots", slots_hbm, slots_ref), ("m1", m1_hbm, m1_ref), ("m2", m2_hbm, m2_ref),
    )
    for n, (name, there, here) in enumerate(pairs):
        loads[name] = pltpu.make_async_copy(there, here, lsem.at[n])
        loads[name].start()

    loads["mw"].wait()
    wown[...] = mw_ref[...].astype(BF16).reshape(2, PART, H)
    is_a = c == 0
    not_a = c == 1

    @pl.when(is_a)
    def _():
        wbuf[y, 0, c] = wown[b]

    def dw_chunk(at):
        cols = pl.ds(pl.multiple_of(at * CH, 128), CH)
        return lax.dot_general(x_ref[:, cols], masked, (((0,), (0,)), ((), ())), preferred_element_type=F32)

    pl.semaphore_wait(barrier, len(near))

    s_wz = sem("wz")
    s_wy = [sem("wy_up", 4), sem("wy_down", 4)]
    s_wsib = sem("wsib", 2)
    send(wown.at[1 - b], wz, s_wz, dev(zz=zq))

    def to_y(rel, here):
        for k in (0, 1):
            send(here, wbuf.at[y, rel, c], s_wy[k] + 2 * rel + c, dev(yy=ys[k], cc=0))

        @pl.when(not_a)
        def _():
            send(here, wbuf.at[y, rel, c], s_wsib + rel, dev(cc=sib))

    to_y(0, wown.at[b])

    loads["hg"].wait()
    s_hg = sem("hg", 7)
    hgall[0, 0, c] = hg_ref[...]
    send(hgall.at[0, 0, c], hgall.at[1, 0, c], s_hg + 2, dev(xx=xp))
    send(hgall.at[0, 0, c], hgall.at[0, 1, c], s_hg + 1, dev(zz=zq))
    send(hgall.at[0, 0, c], hgall.at[0, 0, c], s_hg, dev(cc=sib))
    loads["cnt"].wait()

    row = lax.broadcasted_iota(I32, (ROWS, 32), 0)
    blk = lax.broadcasted_iota(I32, (ROWS, 32), 1)
    within = row - CAP * blk
    alive = (within >= 0) & (within < jnp.minimum(cnt_ref[...], CAP))
    alive = jnp.sum(jnp.where(alive, 1.0, 0.0), axis=1, keepdims=True) > 0.5
    masked = jnp.where(alive, hg_ref[...].astype(F32), 0.0).astype(BF16)

    loads["x"].wait()
    part = SH // 2
    s_rx1 = [sem("rx1_right", 4), sem("rx1_left", 4)]
    s_rx2 = [sem("rx2_right", 4), sem("rx2_left", 4)]
    s_ry1 = [sem("ry1_up"), sem("ry1_down")]
    s_ry2 = [sem("ry2_up"), sem("ry2_down")]
    far_first = (2, 1, 3, 0)

    def yat(d):
        return (y + d) % 4

    sopp[...] = dw_chunk(x2).astype(BF16).reshape(4, 2, part, H)

    def grads_one(k):
        for d in far_first:
            send(sopp.at[yat(d), k], rx1.at[k, yat(d)], s_rx1[0] + 4 * k + d, dev(xx=(x + 1 + 2 * k) % 4))

    grads_one(1 - x % 2)
    b3 = lax.broadcasted_iota(I32, (8, BL, 1), 0)
    w3 = lax.broadcasted_iota(I32, (8, BL, 1), 1)
    r3 = jnp.where(w3 >= 40, 1, 0)
    v3 = w3 - 40 * r3
    l3 = jnp.where(v3 >= 20, 1, 0)
    u3 = v3 - 20 * l3
    c3 = jnp.where(u3 >= 10, 1, 0)
    p3 = u3 - 10 * c3
    z3 = (z + b3) & 7
    source = (r3 * ROWS + (l3 * 16 + z3 * 2 + c3) * CAP + p3).reshape(8 * BL, 1)
    perm = jnp.where(lax.broadcasted_iota(I32, (8 * BL, 2 * ROWS), 1) == source, 1.0, 0.0).astype(BF16)

    for k in (0, 1):
        sside[k] = dw_chunk(xs[k]).astype(BF16).reshape(4, 2, part, H)
    gown[...] = dw_chunk(x).reshape(4, SH, H)

    arrived(wz, s_wz)
    to_y(1, wz)

    @pl.when(is_a)
    def _():
        wbuf[y, 1, c] = wz[...]

    s_wyf = [sem("wyf_up"), sem("wyf_down")]
    s_wx = sem("wx", 4)
    order = (0, 3, 1, 2)

    def half_of(d, k):
        return wbuf.at[yat(d), k]

    def spread(d):
        send(wbuf.at[yat(d)], wbuf.at[yat(d)], s_wx + d, dev(xx=xw, cc=sib))

    def gather_a_first():
        for rel in (0, 1):
            arrived(wbuf.at[y, rel, sib], s_wsib + rel)
        spread(0)

    def gather_a():
        for k, d in ((0, 3), (1, 1)):
            for rel in (0, 1):
                for cc in (0, 1):
                    arrived(wbuf.at[yat(d), rel, cc], s_wy[k] + 2 * rel + cc)
                if rel == k:
                    send(half_of(d, k), half_of(d, k), s_wyf[k], dev(yy=ys[k]))
            spread(d)

    def gather_a_last():
        for k in (0, 1):
            arrived(half_of(2, k), s_wyf[k])
        spread(2)

    def gather_b():
        for d in (0, 3, 1):
            arrived(wbuf.at[yat(d)], s_wx + d)

    def gather_b_last():
        arrived(wbuf.at[y2], s_wx + 2)

    def pass_on():
        sent(hgall.at[0, 0, c], s_hg + 2)
        grads_one(x % 2)
        arrived(hgall.at[1, 0, c], s_hg + 2)
        send(hgall.at[1, 0, c], hgall.at[1, 1, c], s_hg + 4, dev(zz=zq))
        send(hgall.at[1, 0, c], hgall.at[1, 0, c], s_hg + 3, dev(cc=sib))
        arrived(hgall.at[0, 1, c], s_hg + 1)
        send(hgall.at[0, 1, c], hgall.at[0, 1, c], s_hg + 5, dev(cc=sib))

    def sort_rows(rel, cc):
        both = jnp.concatenate([hgall[0, rel, cc], hgall[1, rel, cc]], axis=0)
        hgp[rel, cc] = jnp.dot(perm, both, preferred_element_type=F32).astype(BF16)

    def rows_in():
        arrived(hgall.at[0, 0, sib], s_hg)
        arrived(hgall.at[1, 0, sib], s_hg + 3)
        sort_rows(0, 0)
        sort_rows(0, 1)
        arrived(hgall.at[1, 1, c], s_hg + 4)
        send(hgall.at[1, 1, c], hgall.at[1, 1, c], s_hg + 6, dev(cc=sib))
        arrived(hgall.at[0, 1, sib], s_hg + 5)
        sort_rows(1, c)
        arrived(hgall.at[1, 1, sib], s_hg + 6)
        sort_rows(1, sib)

    s_rows = sem("rows", 8 * n_units)
    s_fin = sem("fin", 8 * n_units)
    far = (4, 3, 5, 2, 6, 1, 7)

    def rows_one(u):
        total = jnp.zeros((8 * BL, WIDTHS[u]), F32)
        for rel in (0, 1):
            for cc in (0, 1):
                pieces = [wbuf[yat(d), rel, cc, pl.ds(at, n)] for d, at, n in UNITS[u]]
                weights = jnp.concatenate(pieces, axis=0)
                total += lax.dot_general(hgp[rel, cc], weights, (((1,), (1,)), ((), ())), preferred_element_type=F32)
        res[u][...] = total.astype(BF16).reshape(8, BL, WIDTHS[u])
        for i in far:
            send(res[u].at[i], rcv[u].at[i % 2, i // 2], s_rows + 8 * u + i, dev(zz=(z + i) % 8))
        rcv[u][0, 0] = res[u][0]

    rr = lax.broadcasted_iota(I32, (256, 4 * BL), 0)
    col = lax.broadcasted_iota(I32, (1, 4 * BL), 1)
    tt = jnp.zeros_like(col)
    for t in (1, 2, 3):
        tt = tt + jnp.where(col >= t * BL, 1, 0)
    ww = col - BL * tt
    gg = jnp.zeros_like(col)
    for g in range(1, 8):
        gg = gg + jnp.where(ww >= g * CAP, 1, 0)

    def sorting(par):
        expert = jnp.where(((z + 16 - 2 * tt - par) & 7) >= 4, 1, 0)
        target = gg * 32 + expert * CAP + ww - CAP * gg
        return jnp.where(rr == target, 1.0, 0.0).astype(BF16)

    owners = [(rep, ll, cc) for rep in (1, 0) for ll in (1 - yl, yl) for cc in (c, sib)]

    def rows_two(u):
        for par in (0, 1):
            for t in range(4):
                i = 2 * t + par
                if i:
                    arrived(rcv[u].at[par, t], s_rows + 8 * u + i)
            rows = jnp.dot(sorting(par), rcv[u][par].reshape(4 * BL, WIDTHS[u]), preferred_element_type=F32)
            outg[u][:, par] = rows.astype(BF16).reshape(8, 32, WIDTHS[u])
        for k, (rep, ll, cc) in enumerate(owners):
            if k == 6:
                fin[u][0, c, yl] = outg[u][yl * 2 + c]
                continue
            send(outg[u].at[rep * 4 + ll * 2 + cc], fin[u].at[rep, c, yl], s_fin + 8 * u + k,
                 dev(xx=(x, xp)[rep], ll=ll, cc=cc), s_fin + 8 * u + 4 * rep + 2 * c + yl)

    def grads_two(*blocks):
        for d in blocks:
            for k in (0, 1):
                arrived(rx1.at[k, yat(d)], s_rx1[k] + d)
                sside[k, yat(d), k] = (sside[k, yat(d), k].astype(F32) + rx1[k, yat(d)].astype(F32)).astype(BF16)
                send(sside.at[k, yat(d)], rx2.at[k, yat(d)], s_rx2[k] + d, dev(xx=xs[k]))

    def side_sent(*blocks):
        for d in blocks:
            for k in (0, 1):
                sent(sside.at[k, yat(d)], s_rx2[k] + d)

    def over_x(d):
        rows = gown[yat(d)]
        for k in (0, 1):
            arrived(rx2.at[k, yat(d)], s_rx2[k] + d)
            rows = rows + rx2[k, yat(d)].reshape(SH, H).astype(F32)
        return rows

    def grads_three():
        ysopp[...] = over_x(2).astype(BF16).reshape(2, part, H)
        for k in (0, 1):
            send(ysopp.at[k], ry1.at[k], s_ry1[k], dev(yy=ys[k]))

    def grads_four():
        for k, d in ((0, 1), (1, 3)):
            rows = over_x(d).reshape(2, part, H)
            arrived(ry1.at[k], s_ry1[k])
            ysside[k, k] = (rows[k] + ry1[k].astype(F32)).astype(BF16)
            ysside[k, 1 - k] = rows[1 - k].astype(BF16)
            send(ysside.at[k], ry2.at[k], s_ry2[k], dev(yy=ys[k]))

    leaves = []

    def adam():
        grads = over_x(0)
        for k in (0, 1):
            arrived(ry2.at[k], s_ry2[k])
        for name in ("m1", "m2"):
            loads[name].wait()
        grads = grads + ry2[0].reshape(SH, H).astype(F32) + ry2[1].reshape(SH, H).astype(F32)
        master = mw_ref[...]
        new_first = beta_one * m1_ref[...] + (1.0 - beta_one) * grads
        new_second = beta_two * m2_ref[...] + (1.0 - beta_two) * grads * grads
        first_hat = new_first / (1.0 - beta_one**step_count)
        second_hat = new_second / (1.0 - beta_two**step_count)
        nw_ref[...] = master - learn_rate * (
            first_hat / (jnp.sqrt(second_hat) + adam_epsilon) + weight_decay * master
        )
        n1_ref[...] = new_first
        n2_ref[...] = new_second
        for n, (here, there) in enumerate(((nw_ref, nw_hbm), (n1_ref, n1_hbm), (n2_ref, n2_hbm))):
            leaves.append(pltpu.make_async_copy(here, there, lsem.at[8 + n]))
            leaves[-1].start()

    @pl.when(is_a)
    def _():
        gather_a_first()
        pass_on()
        gather_a()
        grads_two(2)
        rows_in()
        rows_one(0)
        gather_a_last()
        rows_one(1)
        side_sent(2)
        grads_two(1, 3)

    @pl.when(not_a)
    def _():
        pass_on()
        grads_two(2)
        rows_in()
        gather_b()
        rows_one(0)
        gather_b_last()
        rows_one(1)
        side_sent(2)
        grads_two(1, 3)

    from_col = lax.broadcasted_iota(I32, (PLACES[-1] + WIDTHS[-1], 1), 0)
    belongs = jnp.zeros_like(from_col)
    for u in range(n_units):
        done = PLACES[u]
        for d, at, n in UNITS[u]:
            belongs = jnp.where(from_col >= done, yat(d) * SH + at + from_col - done, belongs)
            done += n
    to_col = lax.broadcasted_iota(I32, (PLACES[-1] + WIDTHS[-1], CH), 1)
    for par in (0, 1):
        rows_of = b if par == 0 else 1 - b
        place[par] = jnp.where(to_col == belongs + rows_of * PART, 1.0, 0.0).astype(BF16)

    grads_three()
    side_sent(1, 3)
    grads_two(0)
    rows_two(0)
    grads_four()
    rows_two(1)
    adam()

    wanted = lax.broadcasted_iota(I32, (64, 128), 0)
    table = jnp.zeros((64, 128), F32)
    loads["ids"].wait()
    loads["slots"].wait()
    for r in range(ids_ref.shape[0]):
        expert_id = ids_ref[pl.ds(r, 1), :]
        slot_id = slots_ref[pl.ds(r, 1), :]
        lower = jnp.where(expert_id >= 2, 1, 0)
        code = lower * 32 + (expert_id - 2 * lower) * CAP + slot_id
        code = jnp.where((slot_id >= 0) & (expert_id < 4), code, -1)
        table = table + jnp.where(wanted == code, 1.0, 0.0)
    table = table.astype(BF16)

    for u in range(n_units):
        for rep in (0, 1):
            for ll in (yl, 1 - yl):
                for cc in (c, sib):
                    if rep == 1 or ll is not yl or cc is not c:
                        arrived(fin[u].at[rep, cc, ll], s_fin + 8 * u + 4 * rep + 2 * cc + ll)
    for rep in (0, 1):
        for cc in (0, 1):
            natural = jnp.zeros((64, CH), F32)
            for u in range(n_units):
                for par in (0, 1):
                    natural += jnp.dot(
                        fin[u][rep, cc, :, par].reshape(64, WIDTHS[u]), place[par, pl.ds(PLACES[u], WIDTHS[u])],
                        preferred_element_type=F32,
                    )
            from_x = (x, xp)[rep]
            chunk = (from_x, 3 - from_x)[cc]
            out_ref[rep, cc] = lax.dot_general(
                table, natural.astype(BF16), (((0,), (0,)), ((), ())), preferred_element_type=F32
            ).astype(BF16)
            there = out_hbm.at[:, pl.ds(pl.multiple_of(chunk * CH, 128), CH)]
            leaves.append(pltpu.make_async_copy(out_ref.at[rep, cc], there, lsem.at[11 + 2 * rep + cc]))
            leaves[-1].start()

    for leaf in leaves:
        leaf.wait()
    for k in (0, 1):
        for rel in (0, 1):
            sent(wz, s_wy[k] + 2 * rel + c)
        for d in order:
            sent(sopp.at[yat(d), k], s_rx1[k] + d)
        sent(sside.at[k, y], s_rx2[k])
        sent(ysopp.at[k], s_ry1[k])
        sent(ysside.at[k], s_ry2[k])
    sent(wz, s_wz)
    for u in range(n_units):
        for i in far:
            sent(res[u].at[i], s_rows + 8 * u + i)
        for k in (0, 1, 2, 3, 4, 5, 7):
            sent(outg[u].at[k], s_fin + 8 * u + k)
    for k in (0, 1, 3, 4, 5, 6):
        sent(hgall.at[0, 0, c], s_hg + k)

    @pl.when(is_a)
    def _():
        for k, d in ((0, 3), (1, 1)):
            sent(half_of(d, k), s_wyf[k])
        for d in order:
            sent(wbuf.at[yat(d)], s_wx + d)

    @pl.when(not_a)
    def _():
        for rel in (0, 1):
            sent(wz, s_wsib + rel)


def hand_over(*refs):
    there, held, back, sems = refs[:4], refs[8:12], refs[4:8], refs[12]
    loads = [pltpu.make_async_copy(there[n], held[n], sems.at[n]) for n in range(4)]
    stores = [pltpu.make_async_copy(held[n], back[n], sems.at[4 + n]) for n in range(4)]
    for load in loads:
        load.start()
    for load, store in zip(loads, stores):
        load.wait()
        store.start()
    for store in stores:
        store.wait()


def body(expert_inputs, hidden_grads, row_counts, top_ids, route_slots, master, first, second):
    hbm = pl.BlockSpec(memory_space=pltpu.HBM)
    shard = jax.ShapeDtypeStruct((SH, H), F32)
    results = pl.pallas_call(
        kernel,
        out_shape=(jax.ShapeDtypeStruct((128, D), BF16), shard, shard, shard),
        in_specs=[hbm] * 8,
        out_specs=(hbm,) * 4,
        scratch_shapes=[
            pltpu.VMEM((2, 2, 128, CH), BF16),
            pltpu.VMEM((SH, H), F32),
            pltpu.VMEM((SH, H), F32),
            pltpu.VMEM((SH, H), F32),
            pltpu.VMEM((ROWS, D), BF16),
            pltpu.VMEM((ROWS, H), BF16),
            pltpu.VMEM((1, 32), I32),
            pltpu.VMEM((8, 128), I32),
            pltpu.VMEM((8, 128), I32),
            pltpu.VMEM((SH, H), F32),
            pltpu.VMEM((SH, H), F32),
            pltpu.VMEM((SH, H), F32),
            pltpu.VMEM((2, PART, H), BF16),
            pltpu.VMEM((PART, H), BF16),
            pltpu.VMEM((4, 2, 2, PART, H), BF16),
            pltpu.VMEM((2, 2, 2, ROWS, H), BF16),
            pltpu.VMEM((2, 2, 8 * BL, H), BF16),
            pltpu.VMEM((2, PLACES[-1] + WIDTHS[-1], CH), BF16),
            pltpu.VMEM((4, 2, SH // 2, H), BF16),
            pltpu.VMEM((2, 4, 2, SH // 2, H), BF16),
            pltpu.VMEM((2, 4, SH // 2, H), BF16),
            pltpu.VMEM((2, 4, 2, SH // 2, H), BF16),
            pltpu.VMEM((2, SH // 2, H), BF16),
            pltpu.VMEM((2, 2, SH // 2, H), BF16),
            pltpu.VMEM((2, SH // 2, H), BF16),
            pltpu.VMEM((2, 2, SH // 2, H), BF16),
            pltpu.VMEM((4, SH, H), F32),
            pltpu.SemaphoreType.DMA((N_SEM,)),
            pltpu.SemaphoreType.DMA((N_SEM,)),
            pltpu.SemaphoreType.DMA((16,)),
            *[pltpu.VMEM((8, BL, n), BF16) for n in WIDTHS],
            *[pltpu.VMEM((2, 4, BL, n), BF16) for n in WIDTHS],
            *[pltpu.VMEM((8, 2, 32, n), BF16) for n in WIDTHS],
            *[pltpu.VMEM((2, 2, 2, 2, 32, n), BF16) for n in WIDTHS],
        ],
        compiler_params=pltpu.CompilerParams(
            collective_id=0, has_side_effects=True, vmem_limit_bytes=56 * 2**20
        ),
    )(
        expert_inputs, hidden_grads, row_counts.reshape(1, 32), top_ids.T, route_slots.T,
        master[0], first[0], second[0],
    )
    out, new_master, new_first, new_second = pl.pallas_call(
        hand_over,
        out_shape=(jax.ShapeDtypeStruct((128, D), BF16), shard, shard, shard),
        in_specs=[hbm] * 4,
        out_specs=(hbm,) * 4,
        scratch_shapes=[
            pltpu.VMEM((128, D), BF16),
            *[pltpu.VMEM((SH, H), F32)] * 3,
            pltpu.SemaphoreType.DMA((8,)),
        ],
        compiler_params=pltpu.CompilerParams(vmem_limit_bytes=56 * 2**20),
    )(*results)
    return out, new_master[None], new_first[None], new_second[None]


def solution(mesh):
    rows = P(("dp", "ep"), None)
    weights = P("ep", "dp", None)
    return jax.shard_map(
        body,
        mesh=mesh,
        in_specs=(rows, rows, P(("dp", "ep")), rows, rows, weights, weights, weights),
        out_specs=(rows, weights, weights, weights),
        check_vma=False,
    )
```

```python
import jax
import jax.numpy as jnp
from jax import lax
from jax.experimental import pallas as pl
from jax.experimental.pallas import tpu as pltpu
from jax.sharding import PartitionSpec as P

MESH = pl.DeviceIdType.MESH
F32 = jnp.float32
BF16 = jnp.bfloat16
I32 = jnp.int32

beta_one = 0.9
beta_two = 0.999
learn_rate = 0.001
adam_epsilon = 1e-08
weight_decay = 0.1
step_count = 100

D = 3584
H = 256
SH = 224
PART = 112
CH = 896
CAP = 10
ROWS = 320
BL = 80
N_SEM = 128
UNITS = (((0, 0, 112), (1, 0, 112), (3, 0, 32)), ((3, 32, 80), (2, 0, 112)))
WIDTHS = tuple(sum(n for _, _, n in unit) for unit in UNITS)
PLACES = tuple(sum(WIDTHS[:u]) for u in range(len(WIDTHS)))


def kernel(
    x_hbm, hg_hbm, cnt_hbm, ids_hbm, slots_hbm, mw_hbm, m1_hbm, m2_hbm,
    out_hbm, nw_hbm, n1_hbm, n2_hbm,
    out_ref, nw_ref, n1_ref, n2_ref,
    x_ref, hg_ref, cnt_ref, ids_ref, slots_ref, mw_ref, m1_ref, m2_ref,
    wown, wz, wbuf, hgall, hgp, place, sopp, sside, rx1, rx2, ysopp, ysside, ry1, ry2, gown,
    ssem, rsem, lsem, *by_unit,
):
    n_units = len(UNITS)
    res, rcv, outg, fin = (by_unit[n_units * n : n_units * (n + 1)] for n in range(4))

    dp = lax.axis_index("dp")
    ep = lax.axis_index("ep")
    x, y = dp // 4, dp % 4
    yl, z, c = ep // 16, (ep // 2) % 8, ep % 2
    b = z % 2
    zq = z + 1 - 2 * b
    sib = 1 - c
    xs = ((x + 1) % 4, (x + 3) % 4)
    ys = ((y + 1) % 4, (y + 3) % 4)
    x2, y2 = (x + 2) % 4, (y + 2) % 4
    xp = x + 1 - 2 * (x % 2)
    xw = 3 - x

    def dev(xx=None, yy=None, ll=None, zz=None, cc=None):
        xx = x if xx is None else xx
        yy = y if yy is None else yy
        ll = yl if ll is None else ll
        zz = z if zz is None else zz
        cc = c if cc is None else cc
        return {"dp": xx * 4 + yy, "ep": ll * 16 + zz * 2 + cc}

    spots = {}
    used = [0]

    def sem(name, many=1):
        if name not in spots:
            spots[name] = used[0]
            used[0] += many
        return spots[name]

    def copy(src, dst, at, to, landing=None):
        return pltpu.make_async_remote_copy(
            src_ref=src, dst_ref=dst, send_sem=ssem.at[at], recv_sem=rsem.at[at if landing is None else landing],
            device_id=to, device_id_type=MESH,
        )

    def arrived(dst, at):
        copy(dst, dst, at, dev(cc=sib)).wait_recv()

    def sent(src, at):
        copy(src, src, at, dev(cc=sib)).wait_send()

    def send(src, dst, at, to, landing=None):
        copy(src, dst, at, to, landing).start()

    barrier = pltpu.get_barrier_semaphore()
    near = [dev(cc=sib), dev(xx=xs[0]), dev(xx=xs[1])]
    near += [dev(yy=yy, cc=cc) for yy in ys for cc in (c, sib)]
    near += [dev(zz=(z + t) % 8) for t in range(1, 8)]
    near += [dev(xx=xp, cc=sib), dev(xx=xw, cc=sib)]
    near += [dev(xx=xx, ll=1 - yl, cc=cc) for xx in (x, xp) for cc in (c, sib)]
    for to in near:
        pl.semaphore_signal(barrier, inc=1, device_id=to, device_id_type=MESH)

    loads = {}
    pairs = (
        ("mw", mw_hbm, mw_ref), ("hg", hg_hbm, hg_ref), ("cnt", cnt_hbm, cnt_ref), ("x", x_hbm, x_ref),
        ("ids", ids_hbm, ids_ref), ("slots", slots_hbm, slots_ref), ("m1", m1_hbm, m1_ref), ("m2", m2_hbm, m2_ref),
    )
    for n, (name, there, here) in enumerate(pairs):
        loads[name] = pltpu.make_async_copy(there, here, lsem.at[n])
        loads[name].start()

    loads["mw"].wait()
    wown[...] = mw_ref[...].astype(BF16).reshape(2, PART, H)
    is_a = c == 0
    not_a = c == 1

    @pl.when(is_a)
    def _():
        wbuf[y, 0, c] = wown[b]

    def dw_chunk(at):
        cols = pl.ds(pl.multiple_of(at * CH, 128), CH)
        return lax.dot_general(x_ref[:, cols], masked, (((0,), (0,)), ((), ())), preferred_element_type=F32)

    pl.semaphore_wait(barrier, len(near))

    s_wz = sem("wz")
    s_wy = [sem("wy_up", 4), sem("wy_down", 4)]
    s_wsib = sem("wsib", 2)
    send(wown.at[1 - b], wz, s_wz, dev(zz=zq))

    def to_y(rel, here):
        for k in (0, 1):
            send(here, wbuf.at[y, rel, c], s_wy[k] + 2 * rel + c, dev(yy=ys[k], cc=0))

        @pl.when(not_a)
        def _():
            send(here, wbuf.at[y, rel, c], s_wsib + rel, dev(cc=sib))

    to_y(0, wown.at[b])

    loads["hg"].wait()
    s_hg = sem("hg", 7)
    hgall[0, 0, c] = hg_ref[...]
    send(hgall.at[0, 0, c], hgall.at[1, 0, c], s_hg + 2, dev(xx=xp))
    send(hgall.at[0, 0, c], hgall.at[0, 1, c], s_hg + 1, dev(zz=zq))
    send(hgall.at[0, 0, c], hgall.at[0, 0, c], s_hg, dev(cc=sib))
    loads["cnt"].wait()

    row = lax.broadcasted_iota(I32, (ROWS, 32), 0)
    blk = lax.broadcasted_iota(I32, (ROWS, 32), 1)
    within = row - CAP * blk
    alive = (within >= 0) & (within < jnp.minimum(cnt_ref[...], CAP))
    alive = jnp.sum(jnp.where(alive, 1.0, 0.0), axis=1, keepdims=True) > 0.5
    masked = jnp.where(alive, hg_ref[...].astype(F32), 0.0).astype(BF16)

    loads["x"].wait()
    part = SH // 2
    s_rx1 = [sem("rx1_right", 4), sem("rx1_left", 4)]
    s_rx2 = [sem("rx2_right", 4), sem("rx2_left", 4)]
    s_ry1 = [sem("ry1_up"), sem("ry1_down")]
    s_ry2 = [sem("ry2_up"), sem("ry2_down")]
    far_first = (2, 1, 3, 0)

    def yat(d):
        return (y + d) % 4

    sopp[...] = dw_chunk(x2).astype(BF16).reshape(4, 2, part, H)

    def grads_one(k):
        for d in far_first:
            send(sopp.at[yat(d), k], rx1.at[k, yat(d)], s_rx1[0] + 4 * k + d, dev(xx=(x + 1 + 2 * k) % 4))

    grads_one(1 - x % 2)
    b3 = lax.broadcasted_iota(I32, (8, BL, 1), 0)
    w3 = lax.broadcasted_iota(I32, (8, BL, 1), 1)
    r3 = jnp.where(w3 >= 40, 1, 0)
    v3 = w3 - 40 * r3
    l3 = jnp.where(v3 >= 20, 1, 0)
    u3 = v3 - 20 * l3
    c3 = jnp.where(u3 >= 10, 1, 0)
    p3 = u3 - 10 * c3
    z3 = (z + b3) & 7
    source = (r3 * ROWS + (l3 * 16 + z3 * 2 + c3) * CAP + p3).reshape(8 * BL, 1)
    perm = jnp.where(lax.broadcasted_iota(I32, (8 * BL, 2 * ROWS), 1) == source, 1.0, 0.0).astype(BF16)

    for k in (0, 1):
        sside[k] = dw_chunk(xs[k]).astype(BF16).reshape(4, 2, part, H)
    gown[...] = dw_chunk(x).reshape(4, SH, H)

    arrived(wz, s_wz)
    to_y(1, wz)

    @pl.when(is_a)
    def _():
        wbuf[y, 1, c] = wz[...]

    s_wyf = [sem("wyf_up"), sem("wyf_down")]
    s_wx = sem("wx", 4)
    order = (0, 3, 1, 2)

    def half_of(d, k):
        return wbuf.at[yat(d), k]

    def spread(d):
        send(wbuf.at[yat(d)], wbuf.at[yat(d)], s_wx + d, dev(xx=xw, cc=sib))

    def gather_a_first():
        for rel in (0, 1):
            arrived(wbuf.at[y, rel, sib], s_wsib + rel)
        spread(0)

    def gather_a():
        for k, d in ((0, 3), (1, 1)):
            for rel in (0, 1):
                for cc in (0, 1):
                    arrived(wbuf.at[yat(d), rel, cc], s_wy[k] + 2 * rel + cc)
                if rel == k:
                    send(half_of(d, k), half_of(d, k), s_wyf[k], dev(yy=ys[k]))
            spread(d)

    def gather_a_last():
        for k in (0, 1):
            arrived(half_of(2, k), s_wyf[k])
        spread(2)

    def gather_b():
        for d in (0, 3, 1):
            arrived(wbuf.at[yat(d)], s_wx + d)

    def gather_b_last():
        arrived(wbuf.at[y2], s_wx + 2)

    def pass_on():
        sent(hgall.at[0, 0, c], s_hg + 2)
        grads_one(x % 2)
        arrived(hgall.at[1, 0, c], s_hg + 2)
        send(hgall.at[1, 0, c], hgall.at[1, 1, c], s_hg + 4, dev(zz=zq))
        send(hgall.at[1, 0, c], hgall.at[1, 0, c], s_hg + 3, dev(cc=sib))
        arrived(hgall.at[0, 1, c], s_hg + 1)
        send(hgall.at[0, 1, c], hgall.at[0, 1, c], s_hg + 5, dev(cc=sib))

    def sort_rows(rel, cc):
        both = jnp.concatenate([hgall[0, rel, cc], hgall[1, rel, cc]], axis=0)
        hgp[rel, cc] = jnp.dot(perm, both, preferred_element_type=F32).astype(BF16)

    def rows_in():
        arrived(hgall.at[0, 0, sib], s_hg)
        arrived(hgall.at[1, 0, sib], s_hg + 3)
        sort_rows(0, 0)
        sort_rows(0, 1)
        arrived(hgall.at[1, 1, c], s_hg + 4)
        send(hgall.at[1, 1, c], hgall.at[1, 1, c], s_hg + 6, dev(cc=sib))
        arrived(hgall.at[0, 1, sib], s_hg + 5)
        sort_rows(1, c)
        arrived(hgall.at[1, 1, sib], s_hg + 6)
        sort_rows(1, sib)

    s_rows = sem("rows", 8 * n_units)
    s_fin = sem("fin", 8 * n_units)
    far = (4, 3, 5, 2, 6, 1, 7)

    def rows_one(u):
        total = jnp.zeros((8 * BL, WIDTHS[u]), F32)
        for rel in (0, 1):
            for cc in (0, 1):
                pieces = [wbuf[yat(d), rel, cc, pl.ds(at, n)] for d, at, n in UNITS[u]]
                weights = jnp.concatenate(pieces, axis=0)
                total += lax.dot_general(hgp[rel, cc], weights, (((1,), (1,)), ((), ())), preferred_element_type=F32)
        res[u][...] = total.astype(BF16).reshape(8, BL, WIDTHS[u])
        for i in far:
            send(res[u].at[i], rcv[u].at[i % 2, i // 2], s_rows + 8 * u + i, dev(zz=(z + i) % 8))
        rcv[u][0, 0] = res[u][0]

    rr = lax.broadcasted_iota(I32, (256, 4 * BL), 0)
    col = lax.broadcasted_iota(I32, (1, 4 * BL), 1)
    tt = jnp.zeros_like(col)
    for t in (1, 2, 3):
        tt = tt + jnp.where(col >= t * BL, 1, 0)
    ww = col - BL * tt
    gg = jnp.zeros_like(col)
    for g in range(1, 8):
        gg = gg + jnp.where(ww >= g * CAP, 1, 0)

    def sorting(par):
        expert = jnp.where(((z + 16 - 2 * tt - par) & 7) >= 4, 1, 0)
        target = gg * 32 + expert * CAP + ww - CAP * gg
        return jnp.where(rr == target, 1.0, 0.0).astype(BF16)

    owners = [(rep, ll, cc) for rep in (1, 0) for ll in (1 - yl, yl) for cc in (c, sib)]

    def rows_two(u):
        for par in (0, 1):
            for t in range(4):
                i = 2 * t + par
                if i:
                    arrived(rcv[u].at[par, t], s_rows + 8 * u + i)
            rows = jnp.dot(sorting(par), rcv[u][par].reshape(4 * BL, WIDTHS[u]), preferred_element_type=F32)
            outg[u][:, par] = rows.astype(BF16).reshape(8, 32, WIDTHS[u])
        for k, (rep, ll, cc) in enumerate(owners):
            if k == 6:
                fin[u][0, c, yl] = outg[u][yl * 2 + c]
                continue
            send(outg[u].at[rep * 4 + ll * 2 + cc], fin[u].at[rep, c, yl], s_fin + 8 * u + k,
                 dev(xx=(x, xp)[rep], ll=ll, cc=cc), s_fin + 8 * u + 4 * rep + 2 * c + yl)

    def grads_two(*blocks):
        for d in blocks:
            for k in (0, 1):
                arrived(rx1.at[k, yat(d)], s_rx1[k] + d)
                sside[k, yat(d), k] = (sside[k, yat(d), k].astype(F32) + rx1[k, yat(d)].astype(F32)).astype(BF16)
                send(sside.at[k, yat(d)], rx2.at[k, yat(d)], s_rx2[k] + d, dev(xx=xs[k]))

    def side_sent(*blocks):
        for d in blocks:
            for k in (0, 1):
                sent(sside.at[k, yat(d)], s_rx2[k] + d)

    def over_x(d):
        rows = gown[yat(d)]
        for k in (0, 1):
            arrived(rx2.at[k, yat(d)], s_rx2[k] + d)
            rows = rows + rx2[k, yat(d)].reshape(SH, H).astype(F32)
        return rows

    def grads_three():
        ysopp[...] = over_x(2).astype(BF16).reshape(2, part, H)
        for k in (0, 1):
            send(ysopp.at[k], ry1.at[k], s_ry1[k], dev(yy=ys[k]))

    def grads_four():
        for k, d in ((0, 1), (1, 3)):
            rows = over_x(d).reshape(2, part, H)
            arrived(ry1.at[k], s_ry1[k])
            ysside[k, k] = (rows[k] + ry1[k].astype(F32)).astype(BF16)
            ysside[k, 1 - k] = rows[1 - k].astype(BF16)
            send(ysside.at[k], ry2.at[k], s_ry2[k], dev(yy=ys[k]))

    leaves = []

    def adam():
        grads = over_x(0)
        for k in (0, 1):
            arrived(ry2.at[k], s_ry2[k])
        for name in ("m1", "m2"):
            loads[name].wait()
        grads = grads + ry2[0].reshape(SH, H).astype(F32) + ry2[1].reshape(SH, H).astype(F32)
        master = mw_ref[...]
        new_first = beta_one * m1_ref[...] + (1.0 - beta_one) * grads
        new_second = beta_two * m2_ref[...] + (1.0 - beta_two) * grads * grads
        first_hat = new_first / (1.0 - beta_one**step_count)
        second_hat = new_second / (1.0 - beta_two**step_count)
        nw_ref[...] = master - learn_rate * (
            first_hat / (jnp.sqrt(second_hat) + adam_epsilon) + weight_decay * master
        )
        n1_ref[...] = new_first
        n2_ref[...] = new_second
        for n, (here, there) in enumerate(((nw_ref, nw_hbm), (n1_ref, n1_hbm), (n2_ref, n2_hbm))):
            leaves.append(pltpu.make_async_copy(here, there, lsem.at[8 + n]))
            leaves[-1].start()

    @pl.when(is_a)
    def _():
        gather_a_first()
        pass_on()
        gather_a()
        grads_two(2)
        rows_in()
        rows_one(0)
        gather_a_last()
        rows_one(1)
        side_sent(2)
        grads_two(1, 3)

    @pl.when(not_a)
    def _():
        pass_on()
        grads_two(2)
        rows_in()
        gather_b()
        rows_one(0)
        gather_b_last()
        rows_one(1)
        side_sent(2)
        grads_two(1, 3)

    from_col = lax.broadcasted_iota(I32, (PLACES[-1] + WIDTHS[-1], 1), 0)
    belongs = jnp.zeros_like(from_col)
    for u in range(n_units):
        done = PLACES[u]
        for d, at, n in UNITS[u]:
            belongs = jnp.where(from_col >= done, yat(d) * SH + at + from_col - done, belongs)
            done += n
    to_col = lax.broadcasted_iota(I32, (PLACES[-1] + WIDTHS[-1], CH), 1)
    for par in (0, 1):
        rows_of = b if par == 0 else 1 - b
        place[par] = jnp.where(to_col == belongs + rows_of * PART, 1.0, 0.0).astype(BF16)

    grads_three()
    side_sent(1, 3)
    grads_two(0)
    wanted = lax.broadcasted_iota(I32, (64, 128), 0)
    table = jnp.zeros((64, 128), F32)
    loads["ids"].wait()
    loads["slots"].wait()
    for r in range(ids_ref.shape[0]):
        expert_id = ids_ref[pl.ds(r, 1), :]
        slot_id = slots_ref[pl.ds(r, 1), :]
        lower = jnp.where(expert_id >= 2, 1, 0)
        code = lower * 32 + (expert_id - 2 * lower) * CAP + slot_id
        code = jnp.where((slot_id >= 0) & (expert_id < 4), code, -1)
        table = table + jnp.where(wanted == code, 1.0, 0.0)
    table = table.astype(BF16)

    def gather_fin(u):
        for rep in (0, 1):
            for ll in (yl, 1 - yl):
                for cc in (c, sib):
                    if rep == 1 or ll is not yl or cc is not c:
                        arrived(fin[u].at[rep, cc, ll], s_fin + 8 * u + 4 * rep + 2 * cc + ll)

    def natural_of(u, rep, cc):
        total = jnp.zeros((64, CH), F32)
        for par in (0, 1):
            total += jnp.dot(
                fin[u][rep, cc, :, par].reshape(64, WIDTHS[u]), place[par, pl.ds(PLACES[u], WIDTHS[u])],
                preferred_element_type=F32,
            )
        return total

    rows_two(0)
    grads_four()
    rows_two(1)
    gather_fin(0)
    early = [natural_of(0, rep, cc) for rep in (0, 1) for cc in (0, 1)]
    adam()

    gather_fin(1)
    for rep in (0, 1):
        for cc in (0, 1):
            natural = early[2 * rep + cc] + natural_of(1, rep, cc)
            from_x = (x, xp)[rep]
            chunk = (from_x, 3 - from_x)[cc]
            out_ref[rep, cc] = lax.dot_general(
                table, natural.astype(BF16), (((0,), (0,)), ((), ())), preferred_element_type=F32
            ).astype(BF16)
            there = out_hbm.at[:, pl.ds(pl.multiple_of(chunk * CH, 128), CH)]
            leaves.append(pltpu.make_async_copy(out_ref.at[rep, cc], there, lsem.at[11 + 2 * rep + cc]))
            leaves[-1].start()

    for leaf in leaves:
        leaf.wait()
    for k in (0, 1):
        for rel in (0, 1):
            sent(wz, s_wy[k] + 2 * rel + c)
        for d in order:
            sent(sopp.at[yat(d), k], s_rx1[k] + d)
        sent(sside.at[k, y], s_rx2[k])
        sent(ysopp.at[k], s_ry1[k])
        sent(ysside.at[k], s_ry2[k])
    sent(wz, s_wz)
    for u in range(n_units):
        for i in far:
            sent(res[u].at[i], s_rows + 8 * u + i)
        for k in (0, 1, 2, 3, 4, 5, 7):
            sent(outg[u].at[k], s_fin + 8 * u + k)
    for k in (0, 1, 3, 4, 5, 6):
        sent(hgall.at[0, 0, c], s_hg + k)

    @pl.when(is_a)
    def _():
        for k, d in ((0, 3), (1, 1)):
            sent(half_of(d, k), s_wyf[k])
        for d in order:
            sent(wbuf.at[yat(d)], s_wx + d)

    @pl.when(not_a)
    def _():
        for rel in (0, 1):
            sent(wz, s_wsib + rel)


def hand_over(*refs):
    there, held, back, sems = refs[:4], refs[8:12], refs[4:8], refs[12]
    loads = [pltpu.make_async_copy(there[n], held[n], sems.at[n]) for n in range(4)]
    stores = [pltpu.make_async_copy(held[n], back[n], sems.at[4 + n]) for n in range(4)]
    for load in loads:
        load.start()
    for load, store in zip(loads, stores):
        load.wait()
        store.start()
    for store in stores:
        store.wait()


def body(expert_inputs, hidden_grads, row_counts, top_ids, route_slots, master, first, second):
    hbm = pl.BlockSpec(memory_space=pltpu.HBM)
    shard = jax.ShapeDtypeStruct((SH, H), F32)
    results = pl.pallas_call(
        kernel,
        out_shape=(jax.ShapeDtypeStruct((128, D), BF16), shard, shard, shard),
        in_specs=[hbm] * 8,
        out_specs=(hbm,) * 4,
        scratch_shapes=[
            pltpu.VMEM((2, 2, 128, CH), BF16),
            pltpu.VMEM((SH, H), F32),
            pltpu.VMEM((SH, H), F32),
            pltpu.VMEM((SH, H), F32),
            pltpu.VMEM((ROWS, D), BF16),
            pltpu.VMEM((ROWS, H), BF16),
            pltpu.VMEM((1, 32), I32),
            pltpu.VMEM((8, 128), I32),
            pltpu.VMEM((8, 128), I32),
            pltpu.VMEM((SH, H), F32),
            pltpu.VMEM((SH, H), F32),
            pltpu.VMEM((SH, H), F32),
            pltpu.VMEM((2, PART, H), BF16),
            pltpu.VMEM((PART, H), BF16),
            pltpu.VMEM((4, 2, 2, PART, H), BF16),
            pltpu.VMEM((2, 2, 2, ROWS, H), BF16),
            pltpu.VMEM((2, 2, 8 * BL, H), BF16),
            pltpu.VMEM((2, PLACES[-1] + WIDTHS[-1], CH), BF16),
            pltpu.VMEM((4, 2, SH // 2, H), BF16),
            pltpu.VMEM((2, 4, 2, SH // 2, H), BF16),
            pltpu.VMEM((2, 4, SH // 2, H), BF16),
            pltpu.VMEM((2, 4, 2, SH // 2, H), BF16),
            pltpu.VMEM((2, SH // 2, H), BF16),
            pltpu.VMEM((2, 2, SH // 2, H), BF16),
            pltpu.VMEM((2, SH // 2, H), BF16),
            pltpu.VMEM((2, 2, SH // 2, H), BF16),
            pltpu.VMEM((4, SH, H), F32),
            pltpu.SemaphoreType.DMA((N_SEM,)),
            pltpu.SemaphoreType.DMA((N_SEM,)),
            pltpu.SemaphoreType.DMA((16,)),
            *[pltpu.VMEM((8, BL, n), BF16) for n in WIDTHS],
            *[pltpu.VMEM((2, 4, BL, n), BF16) for n in WIDTHS],
            *[pltpu.VMEM((8, 2, 32, n), BF16) for n in WIDTHS],
            *[pltpu.VMEM((2, 2, 2, 2, 32, n), BF16) for n in WIDTHS],
        ],
        compiler_params=pltpu.CompilerParams(
            collective_id=0, has_side_effects=True, vmem_limit_bytes=56 * 2**20
        ),
    )(
        expert_inputs, hidden_grads, row_counts.reshape(1, 32), top_ids.T, route_slots.T,
        master[0], first[0], second[0],
    )
    out, new_master, new_first, new_second = pl.pallas_call(
        hand_over,
        out_shape=(jax.ShapeDtypeStruct((128, D), BF16), shard, shard, shard),
        in_specs=[hbm] * 4,
        out_specs=(hbm,) * 4,
        scratch_shapes=[
            pltpu.VMEM((128, D), BF16),
            *[pltpu.VMEM((SH, H), F32)] * 3,
            pltpu.SemaphoreType.DMA((8,)),
        ],
        compiler_params=pltpu.CompilerParams(vmem_limit_bytes=56 * 2**20),
    )(*results)
    return out, new_master[None], new_first[None], new_second[None]


def solution(mesh):
    rows = P(("dp", "ep"), None)
    weights = P("ep", "dp", None)
    return jax.shard_map(
        body,
        mesh=mesh,
        in_specs=(rows, rows, P(("dp", "ep")), rows, rows, weights, weights, weights),
        out_specs=(rows, weights, weights, weights),
        check_vma=False,
    )
```
